768 devices in a mesh: tm: 12 (over z), head: 64 (over x, y, core).
Axes of the slice: x: 4, y: 8, z: 12, core: 2. Of those that a mesh axis runs over, the one named last changes fastest.
Arguments:
- xs: bfloat16 [12288, 4096], P('tm', 'head'), may hold values from -6 to 6
- bc: bfloat16 [12288, 256], P('tm'), may hold values from -0.16894531 to 0.16894531
- log_decay: float32 [12288, 64], P('tm', 'head'), may hold values from -1 to 0
- out_grad: bfloat16 [12288, 4096], P('tm', 'head'), may hold values from -6 to 6
- news_owner: int32 [384, 1], P('tm'), may hold values from 0 to 11; in each aligned block of 32 rows (0 to 31, 32 to 63, ...) at most 6 rows name the same one
- news_local: int32 [384, 1], P('tm'), may hold values from 0 to 63
Outputs:
- x_grad: bfloat16 [12288, 4096], P('tm', 'head')
- bc_grad: float32 [12288, 256], P(('tm', 'head'))
- decay_grad: float32 [12288, 64], P('tm', 'head')
- news_grad: float32 [768, 4096], P('tm', 'head')
The draws below stay inside these ranges and needn't reach their ends.
Inputs may be any that keep to these rules, and one draw needn't show every extreme that they name: `news_owner`: among the groups of events of one index of tm, at most 6 name the same owner; in every draw some owner is named by exactly 6 of one index's groups.
All inputs are finite; a program needn't handle non-finite values.
Results may differ from the reference program's by a relative error of at most 0.0012.
Values sent between devices are 32-bit elements; how exact they have to be, the bound alone decides.
A program may use at most 32 MiB of HBM per device.

```python
import math
import jax
import jax.numpy as jnp
import numpy as np
from jax import lax

P_SIZE = 64
N = 128
T_DEV = 1024
NQ = 32
NEWS_DEV = 64
RECURRENT_GROUPS = 64
SEQ = 12288
STRETCHES = 384
NEWS_ROWS = 768
CAP = 6
N_TM = 12


def draw_log_decay(key, part):
    sampler_seeds = jax.random.split(key, 8)
    division_number = SEQ // T_DEV
    heads_draw = jax.random.uniform(sampler_seeds[0], (RECURRENT_GROUPS,))
    share = 0.5
    quick_route = heads_draw < share
    floor_amount = jnp.where(quick_route, 1.0 / 30.0, 0.15 / SEQ) * jnp.exp(jax.random.uniform(sampler_seeds[1], (RECURRENT_GROUPS,), minval=0.0, maxval=math.log(2.0)))
    division_frequency = jnp.exp(jax.random.uniform(sampler_seeds[2], (division_number, 1), minval=math.log(0.5), maxval=math.log(2.0)))
    division_frequency = jnp.repeat(division_frequency, T_DEV, axis=0)
    jitter_shift = jax.random.uniform(sampler_seeds[3], (SEQ, RECURRENT_GROUPS), minval=0.3, maxval=1.7)
    streak_span = max(1, T_DEV // 8)
    run_start = jax.random.randint(sampler_seeds[6], (division_number, RECURRENT_GROUPS), 0, T_DEV - streak_span + 1)
    run_start = jnp.repeat(run_start, T_DEV, axis=0)
    within = (jnp.arange(SEQ) % T_DEV)[:, None]
    within_streak = (within >= run_start) & (within < run_start + streak_span)
    cluster_number = 0.25 / division_number * jnp.exp(jax.random.uniform(sampler_seeds[7], (RECURRENT_GROUPS,), minval=0.0, maxval=math.log(2.0)))
    cluster_extent = jnp.where(within_streak & jnp.logical_not(quick_route)[None, :], cluster_number[None, :] / streak_span, 0.0)
    arrival_frequency = (floor_amount[None, :] + cluster_extent) * division_frequency * jitter_shift
    places = jax.random.randint(sampler_seeds[4], (3,), 0, SEQ)
    struck = jnp.any(jnp.arange(SEQ)[:, None] == places[None, :], axis=1)
    drop = jax.random.uniform(sampler_seeds[5], (SEQ, 1), minval=math.log(0.6), maxval=math.log(0.8))
    return (-arrival_frequency + jnp.where(struck[:, None], drop, 0.0)).astype(jnp.float32)


def plant(array, own_key, low, largest):
    longest = array.shape.index(max(array.shape))
    spots = []
    for shift in (0, 1):
        where = [jax.random.randint(jax.random.fold_in(own_key, axis), (), 0, length) for axis, length in enumerate(array.shape)]
        where[longest] = (where[longest] + shift) % array.shape[longest]
        spots.append(tuple(where))
    return array.at[spots[0]].set(low).at[spots[1]].set(largest)


def shard_levels(rng, dims, shards, smallest, largest):
    loudness = 1.0
    for axis_at, shards_of in shards:
        steps = jax.random.uniform(jax.random.fold_in(jax.random.fold_in(rng, 6), axis_at), (shards_of,), jnp.float32, smallest / len(shards), largest / len(shards))
        loudness = loudness * jnp.repeat(jnp.exp(steps), dims[axis_at] // shards_of).reshape((-1,) + (1,) * (len(dims) - 1 - axis_at))
    return loudness


def shared_out(stream_key, own, number, rows, number_of, top, most, slope):
    ranking = jax.random.permutation(stream_key, number_of)
    heavy_load, usual = shares(number_of, rows * top, most, slope, True), shares(number_of, rows * top, most, slope, False)
    places = jnp.arange(number_of)

    def named(sizes, offset_by):
        used = int((sizes > 0).sum())
        fixed = max(1, used // 4)
        passed = fixed + (places - fixed + offset_by * (used - fixed)) % max(1, number_of - fixed)
        return jnp.zeros((number_of,), jnp.int32).at[ranking[jnp.where(places < fixed, places, passed)]].set(jnp.asarray(sizes, jnp.int32))

    sizes = jnp.where(number % 4 == 0, named(heavy_load, number // 4), named(usual, number - number // 4 - 1))
    mixed = jax.random.permutation(jax.random.fold_in(own, 3), number_of)
    source_of, receiver = mixed[0:number_of // 2 * 2:2], mixed[1:number_of // 2 * 2:2]
    room = jnp.minimum(sizes[source_of] - 1, most - sizes[receiver]) // 2
    room = jnp.where((source_of == ranking[0]) | (receiver == ranking[0]) | (sizes[receiver] == 0), 0, jnp.maximum(room, 0))
    passed = jax.random.randint(jax.random.fold_in(own, 4), (number_of // 2,), 0, 1 << 20) % (room + 1)
    sizes = sizes.at[source_of].add(-passed).at[receiver].add(passed)
    items = jnp.searchsorted(jnp.cumsum(sizes), jnp.arange(rows * top), side="right").astype(jnp.int32)
    table = items.reshape(top, rows).T
    table = table[jax.random.permutation(jax.random.fold_in(own, 1), rows)]
    offset_by = jax.random.randint(jax.random.fold_in(own, 2), (rows, 1), 0, top)
    return jnp.take_along_axis(table, (jnp.arange(top)[None, :] + offset_by) % top, axis=1)


def shares(count, total, reach, skew, full):
    loads = [(1 << 20) // math.isqrt(rank ** skew) + 1 for rank in range(1, count + 1)]
    largest = reach if full else min(reach, max(-(-total // count), total * loads[0] // sum(loads)))
    least = 1 if total - largest >= count - 1 else 0
    counts, rest = [largest] + [least] * (count - 1), total - largest - least * (count - 1)
    while rest > 0:
        movable = [i for i in range(1, count) if counts[i] < largest] or [i for i in range(1, count) if counts[i] < reach]
        mass, left = sum([loads[i] for i in movable]), rest
        for i in movable:
            addition = min(reach - counts[i], max(1, left * loads[i] // mass), rest)
            counts[i] = counts[i] + addition
            rest = rest - addition
    return np.array(counts)


def bell_draw(own_key, extent, spread, bound, shards=(), held_as=jnp.bfloat16):
    entries = jax.random.normal(own_key, extent, jnp.float32) * spread
    if len(shards) > 0:
        entries = shard_levels(own_key, extent, shards, -0.22, 0.18) * entries
    return jnp.clip(entries, min=-bound, max=bound).astype(held_as)


def setup_inputs(seed: int = 0) -> dict:
    seeds = jax.random.split(jax.random.key(seed), 7)
    xs = bell_draw(seeds[0], (SEQ, RECURRENT_GROUPS * P_SIZE), 1.0, 6.0, ((0, 12), (1, 64)))
    bc = bell_draw(seeds[1], (SEQ, 2 * N), (1.0 / (N * SEQ) ** 0.25), 0.16894531, ((0, 12),))
    log_decay = draw_log_decay(jax.random.fold_in(seeds[6], 71), 0)
    out_grad = bell_draw(seeds[3], (SEQ, RECURRENT_GROUPS * P_SIZE), 1.0, 6.0, ((0, 12), (1, 64)))
    news_owner_keys = jax.random.split(jax.random.fold_in(seeds[4], 1), STRETCHES // (T_DEV // NQ))
    news_owner_turns = jax.random.permutation(jax.random.fold_in(seeds[4], 3), STRETCHES // (T_DEV // NQ))
    news_owner = jax.vmap(lambda own, number: shared_out(jax.random.fold_in(seeds[4], 2), own, number, T_DEV // NQ, N_TM, 1, CAP, 2))(news_owner_keys, news_owner_turns).reshape((STRETCHES, 1))
    news_local = plant(jax.random.randint(seeds[5], (STRETCHES, 1), 0, NEWS_DEV), jax.random.fold_in(seeds[5], 1), 0, NEWS_DEV - 1).astype(jnp.int32)
    return {"xs": xs, "bc": bc, "log_decay": log_decay, "out_grad": out_grad, "news_owner": news_owner, "news_local": news_local}


def reference(xs, bc, log_decay, out_grad, news_owner, news_local):
    hp = lax.Precision.HIGHEST
    seq = xs.shape[0]
    heads = log_decay.shape[1]
    width = xs.shape[1] // heads
    state = bc.shape[1] // 2
    inputs = xs.astype(jnp.float32).reshape(seq, heads, width)
    grads = out_grad.astype(jnp.float32).reshape(seq, heads, width)
    bmat = bc[:, :state].astype(jnp.float32)
    cmat = bc[:, state:].astype(jnp.float32)
    decay = jnp.exp(log_decay)
    block_len = 64
    blocks = seq // block_len

    def blocked(arr):
        return arr.reshape((blocks, block_len) + arr.shape[1:])

    decay_b, b_b, c_b, x_b, d_b = blocked(decay), blocked(bmat), blocked(cmat), blocked(inputs), blocked(grads)

    def step_fwd(hcur, inp):
        a_t, b_t, x_t = inp
        hnew = a_t[:, None, None] * hcur + b_t[None, :, None] * x_t[:, None, :]
        return hnew, hcur

    def block_fwd(hcur, inp):
        hnew, _ = lax.scan(step_fwd, hcur, inp)
        return hnew, hcur

    zeros = jnp.zeros((heads, state, width), jnp.float32)
    _, starts = lax.scan(block_fwd, zeros, (decay_b, b_b, x_b))

    def block_back(gnext, inp):
        start, a_blk, b_blk, c_blk, x_blk, d_blk = inp
        _, prevs = lax.scan(step_fwd, start, (a_blk, b_blk, x_blk))

        def back(gn, item):
            hprev, a_t, b_t, c_t, x_t, d_t = item
            gcur = c_t[None, :, None] * d_t[:, None, :] + gn
            hcur = a_t[:, None, None] * hprev + b_t[None, :, None] * x_t[:, None, :]
            dx_t = jnp.einsum('n,hnp->hp', b_t, gcur, precision=hp)
            db_t = jnp.einsum('hnp,hp->n', gcur, x_t, precision=hp)
            dc_t = jnp.einsum('hnp,hp->n', hcur, d_t, precision=hp)
            dla_t = a_t * jnp.sum(gcur * hprev, axis=(1, 2))
            return a_t[:, None, None] * gcur, (dx_t, db_t, dc_t, dla_t)

        gfirst, outs = lax.scan(back, gnext, (prevs, a_blk, b_blk, c_blk, x_blk, d_blk), reverse=True)
        return gfirst, outs

    _, (dx, db, dc, dla) = lax.scan(block_back, zeros, (starts, decay_b, b_b, c_b, x_b, d_b), reverse=True)
    dx = dx.reshape(seq, heads * width)
    db = db.reshape(seq, state)
    dc = dc.reshape(seq, state)
    dla = dla.reshape(seq, heads)
    sums = dx.reshape(seq // NQ, NQ, heads * width).sum(axis=1)
    rows = news_owner[:, 0] * NEWS_DEV + news_local[:, 0]
    news_grad = jnp.zeros((NEWS_ROWS, heads * width), jnp.float32).at[rows].add(sums)
    return dx.astype(jnp.bfloat16), jnp.concatenate([db, dc], axis=1), dla, news_grad
```

```python
import functools

import jax
import jax.numpy as jnp
from jax import lax
from jax.experimental import pallas as pl
from jax.experimental.pallas import tpu as pltpu
from jax.sharding import PartitionSpec as P

MESH = pl.DeviceIdType.MESH
F32 = jnp.float32
BF16 = jnp.bfloat16
NEWS_DEV = 64
NQ = 32
L = 128


def nn(a, b):
    return lax.dot_general(a, b, (((1,), (0,)), ((), ())), preferred_element_type=F32)


def nt(a, b):
    return lax.dot_general(a, b, (((1,), (1,)), ((), ())), preferred_element_type=F32)


def split2(v):
    hi = v.astype(BF16)
    return hi, (v - hi.astype(F32)).astype(BF16)


def split3(v):
    one = v.astype(BF16).astype(F32)
    two = (v - one).astype(BF16).astype(F32)
    return one, two, v - one - two


def iota(shape, dim):
    return lax.broadcasted_iota(jnp.int32, shape, dim)


class Plan:
    def __init__(self, tm, x, y, slots):
        self.tm, self.x, self.y, self.slots = tm, x, y, slots
        self.thirds = tm % 3 == 0
        self.owners = tm // 3 * 2 if self.thirds else tm
        self.rows = 64 // self.owners
        self.block = 1024 // (x * y * 2)
        self.blocks = L // (2 * self.block)

    def is_owner(self, z):
        return lax.rem(z, 3) != 2 if self.thirds else z >= 0

    def owner(self, z):
        return (z // 3) * 2 + lax.rem(z, 3) if self.thirds else z

    def owner_z(self, q):
        return (q // 2) * 3 + q % 2 if self.thirds else q


def kernel(
    plan,
    x_hbm, dy_hbm, bc_hbm, la_hbm, own_hbm, loc_hbm,
    xg_ref, bcg_ref, dla_ref, news_ref,
    xv, dyv, bcv, lav, ownv, locv,
    xd, dyd, acol, bcol, st_loc, ca_loc, pre_b, suf_b, rows_v,
    loc_bc, dbc, crecv, csum, xr1, xr2, ysum, yrecv,
    y_loc, dx_loc, st2, ca2, place_v, ids_v, ve,
    dec_s, dec_r, zs, zr, zo, zb, ns, nr,
    in_sem, dec_ss, dec_rs, z1_ss, z1_rs, z2_ss, z2_rs,
    c_ss, c_rs, x1_ss, x1_rs, x2_ss, x2_rs, y_ss, y_rs, n_ss, n_rs,
):
    nz, ny, nx = plan.tm, plan.y, plan.x
    zi = lax.axis_index("tm")
    hi_ = lax.axis_index("head")
    core = lax.rem(hi_, 2)
    yi = lax.rem(hi_ // 2, ny)
    xi = hi_ // (2 * ny)

    def head(x, y, c):
        return (x * ny + y) * 2 + c

    def at_z(z):
        return (z, hi_)

    def at_head(h):
        return (zi, h)

    right = at_head(head(lax.rem(xi + 1, nx), yi, core))
    left = at_head(head(lax.rem(xi + nx - 1, nx), yi, core))
    twin = at_head(head(xi, yi, 1 - core))

    loads = [
        pltpu.make_async_copy(src, dst, in_sem.at[k])
        for k, (src, dst) in enumerate(
            ((la_hbm, lav), (x_hbm, xv), (bc_hbm, bcv), (dy_hbm, dyv), (own_hbm, ownv), (loc_hbm, locv))
        )
    ]
    for load in loads:
        load.start()

    barrier = pltpu.get_barrier_semaphore()
    greeted = [at_z(lax.rem(zi + d, nz)) for d in range(1, nz)]
    greeted += [twin, left, right]
    greeted += [at_head(head(xi, lax.rem(yi + d, ny), core)) for d in range(1, ny)]
    for device in greeted:
        pl.semaphore_signal(barrier, inc=1, device_id=device, device_id_type=MESH)

    up = jnp.where(iota((L, L), 0) <= iota((L, L), 1), 1.0, 0.0).astype(BF16)
    down = jnp.where(iota((L, L), 0) >= iota((L, L), 1), 1.0, 0.0).astype(BF16)
    loads[0].wait()
    parts = split3(lav[...])
    sums = nn(jnp.concatenate([*parts, jnp.zeros((8, L), F32)], axis=0).astype(BF16), up)
    cums = sums[0:8] + sums[8:16] + sums[16:24]
    tot = jnp.broadcast_to(cums[:, L - 1 : L], (8, L))
    after = jnp.exp(cums)
    before = jnp.exp(tot - cums)
    chunk_decay = jnp.exp(tot)
    tots = [tot[c : c + 1] for c in range(8)]
    run = jnp.zeros((1, L), F32)
    for c in range(8):
        pre_b[c] = jnp.broadcast_to(jnp.exp(run), (8, L))
        run = run + tots[c]
    device_decay = jnp.exp(run)
    run = jnp.zeros((1, L), F32)
    for c in reversed(range(8)):
        suf_b[c] = jnp.broadcast_to(jnp.exp(run), (8, L))
        run = run + tots[c]
    dec_s[...] = device_decay
    dec_r[zi] = device_decay

    pl.semaphore_wait(barrier, len(greeted))

    def dec_copy(d):
        to = lax.rem(zi + d, nz)
        return to, pltpu.make_async_remote_copy(
            src_ref=dec_s, dst_ref=dec_r.at[zi], send_sem=dec_ss.at[d], recv_sem=dec_rs.at[zi],
            device_id=at_z(to), device_id_type=MESH,
        )

    for d in range(1, nz):
        to, copy = dec_copy(d)
        pl.when(plan.is_owner(to))(copy.start)

    loads[1].wait()
    loads[2].wait()
    state = jnp.zeros((64, L), F32)
    for c in range(8):
        part = slice(c * L, (c + 1) * L)
        hi, lo = split2(xv[:, part].astype(F32) * before[c : c + 1])
        bm = bcv[part, 0:L]
        st_loc[c] = state
        state = state * chunk_decay[c : c + 1] + nn(
            jnp.concatenate([hi, lo], axis=1), jnp.concatenate([bm, bm], axis=0)
        )
    st_loc[8] = state
    loads[3].wait()
    back = jnp.zeros((64, L), F32)
    for c in reversed(range(8)):
        part = slice(c * L, (c + 1) * L)
        hi, lo = split2(dyv[:, part].astype(F32) * after[c : c + 1])
        cm = bcv[part, L : 2 * L]
        ca_loc[c] = back
        back = back * chunk_decay[c : c + 1] + nn(
            jnp.concatenate([hi, lo], axis=1), jnp.concatenate([cm, cm], axis=0)
        )
    zs[:, 0] = state.reshape(plan.owners, plan.rows, L)
    zs[:, 1] = back.reshape(plan.owners, plan.rows, L)

    def z1_copy(d):
        to = lax.rem(zi + d, nz)
        return to, pltpu.make_async_remote_copy(
            src_ref=zs.at[plan.owner(to)], dst_ref=zr.at[zi], send_sem=z1_ss.at[d], recv_sem=z1_rs.at[zi],
            device_id=at_z(to), device_id_type=MESH,
        )

    for d in range(1, nz):
        to, copy = z1_copy(d)

        @pl.when(plan.is_owner(to))
        def _():
            copy.start()

    big = jnp.concatenate([cums, after, before, jnp.zeros((L - 24, L), F32)], axis=0).T
    lower = iota((L, L), 0) >= iota((L, L), 1)
    upper = iota((L, L), 0) <= iota((L, L), 1)
    rows_v[0] = after
    rows_v[1] = before

    def local(c):
        part = slice(c * L, (c + 1) * L)
        bm, cm = bcv[part, 0:L], bcv[part, L : 2 * L]
        xt, dyt = xv[:, part], dyv[:, part]
        xf, dyf = xt.astype(F32), dyt.astype(F32)
        x2 = jnp.concatenate([xf, xf], axis=0).T.astype(BF16)
        dy2 = jnp.concatenate([dyf, dyf], axis=0).T.astype(BF16)
        xd[c] = x2
        dyd[c] = dy2
        col = jnp.broadcast_to(big[:, c : c + 1], (L, L))
        acol[c] = jnp.broadcast_to(big[:, 8 + c : 9 + c], (L, L))
        bcol[c] = jnp.broadcast_to(big[:, 16 + c : 17 + c], (L, L))
        row = jnp.broadcast_to(cums[c : c + 1], (L, L))
        m = jnp.exp(jnp.where(lower, col - row, -1e30))
        mt = jnp.exp(jnp.where(upper, row - col, -1e30))
        w = split2(m * nt(cm, bm))
        q = split2(m * nn(dy2[:, 0:64], xt))
        qt = split2(mt * nn(x2[:, 0:64], dyt))
        loc_bc[c, :, 0:L] = nn(jnp.concatenate(qt, axis=1), jnp.concatenate([cm, cm], axis=0))
        loc_bc[c, :, L : 2 * L] = nn(jnp.concatenate(q, axis=1), jnp.concatenate([bm, bm], axis=0))
        y_loc[c] = nt(jnp.concatenate([xt, xt], axis=1), jnp.concatenate(w, axis=1))
        dx_loc[c] = nn(jnp.concatenate([dyt, dyt], axis=1), jnp.concatenate(w, axis=0))

    for c in range(4):
        local(c)

    @pl.when(plan.is_owner(zi))
    def _():
        zr[zi] = zs[plan.owner(zi)]
        for d in range(1, nz):
            source = lax.rem(zi + nz - d, nz)
            pltpu.make_async_remote_copy(
                src_ref=dec_s, dst_ref=dec_r.at[source], send_sem=dec_ss.at[d], recv_sem=dec_rs.at[source],
                device_id=at_z(source), device_id_type=MESH,
            ).wait_recv()
            pltpu.make_async_remote_copy(
                src_ref=zs.at[0], dst_ref=zr.at[source], send_sem=z1_ss.at[d], recv_sem=z1_rs.at[source],
                device_id=at_z(source), device_id_type=MESH,
            ).wait_recv()
        run = jnp.zeros((plan.rows, L), F32)
        for j in range(nz):
            zo[j, 0] = run
            run = run * dec_r[j] + zr[j, 0]
        run = jnp.zeros((plan.rows, L), F32)
        for j in reversed(range(nz)):
            zo[j, 1] = run
            run = run * dec_r[j] + zr[j, 1]
        mine = plan.owner(zi)
        for d in range(1, nz):
            to = lax.rem(zi + d, nz)
            pltpu.make_async_remote_copy(
                src_ref=zo.at[to], dst_ref=zb.at[mine], send_sem=z2_ss.at[d], recv_sem=z2_rs.at[mine],
                device_id=at_z(to), device_id_type=MESH,
            ).start()
        zb[mine] = zo[zi]

    for c in range(4, 8):
        local(c)
    ns_rows = nz * plan.slots
    loads[4].wait()
    loads[5].wait()
    owner_row = ownv[...]
    named = jnp.where(iota((16, NQ), 0) == owner_row, 1.0, 0.0)
    earlier = jnp.where(iota((NQ, NQ), 0) < iota((NQ, NQ), 1), 1.0, 0.0)
    rank = jnp.sum(named * nn(named.astype(BF16), earlier.astype(BF16)), axis=0, keepdims=True)
    slot = owner_row.astype(F32) * plan.slots + rank
    spread = jnp.where(iota((NQ, 1024), 0) == iota((NQ, 1024), 1) // NQ, 1.0, 0.0).astype(BF16)
    slot_t = nn(jnp.broadcast_to(slot, (16, NQ)).astype(BF16), spread)
    for c in range(8):
        hit = slot_t[0:1, c * L : (c + 1) * L] == iota((ns_rows, L), 0).astype(F32)
        place_v[c] = jnp.where(hit, 1.0, 0.0).astype(BF16)
    hit = slot == iota((ns_rows, NQ), 0).astype(F32)
    ids = jnp.sum(jnp.where(hit, locv[...].astype(F32) + 1.0, 0.0), axis=1, keepdims=True)
    ids_v[...] = jnp.where(iota((ns_rows, L), 1) >= 64, ids, 0.0)

    for q in range(plan.owners):
        source = plan.owner_z(q)

        @pl.when(source != zi)
        def _():
            pltpu.make_async_remote_copy(
                src_ref=zo.at[0], dst_ref=zb.at[q], send_sem=z2_ss.at[0], recv_sem=z2_rs.at[q],
                device_id=at_z(source), device_id_type=MESH,
            ).wait_recv()

    start = zb[:, 0].reshape(64, L)
    carry = zb[:, 1].reshape(64, L)

    def with_edge(local_state, scale, edge):
        return local_state + (edge.reshape(8, 8, L) * scale[None]).reshape(64, L)

    def core_copy(c, k):
        return pltpu.make_async_remote_copy(
            src_ref=dbc.at[c, :, 1 - core], dst_ref=crecv.at[c], send_sem=c_ss.at[k], recv_sem=c_rs.at[k],
            device_id=twin, device_id_type=MESH,
        )

    def finish_bc(c, k):
        st = jnp.concatenate(split2(with_edge(st_loc[c], pre_b[c], start)), axis=0)
        ca = jnp.concatenate(split2(with_edge(ca_loc[c], suf_b[c], carry)), axis=0)
        st2[c] = st
        ca2[c] = ca
        shape = (plan.blocks, 2, plan.block, L)
        dbc[c, :, :, :, 0:L] = (loc_bc[c, :, 0:L] + bcol[c] * nn(xd[c], ca)).reshape(shape)
        dbc[c, :, :, :, L : 2 * L] = (loc_bc[c, :, L : 2 * L] + acol[c] * nn(dyd[c], st)).reshape(shape)
        core_copy(c, k).start()

    far = lax.rem(xi + 2, nx)
    east = lax.rem(xi + 1, nx)
    west = lax.rem(xi + nx - 1, nx)
    order = [2 * far, 2 * far + 1, 2 * east + 1, 2 * west, 2 * east, 2 * west + 1, 2 * xi, 2 * xi + 1]
    for k, c in enumerate(order):
        finish_bc(c, k)

    def core_sum(k):
        c = order[k]
        core_copy(c, k).wait_recv()
        csum[k] = dbc[c, :, core] + crecv[c]

    def x_copy(k, dst, sems, r, device):
        return pltpu.make_async_remote_copy(
            src_ref=csum.at[k], dst_ref=dst.at[r], send_sem=sems[0].at[r], recv_sem=sems[1].at[r],
            device_id=device, device_id_type=MESH,
        )

    x1 = [x_copy(0, xr1, (x1_ss, x1_rs), 0, right), x_copy(1, xr1, (x1_ss, x1_rs), 1, left)]
    x2 = [
        x_copy(2, xr2, (x2_ss, x2_rs), 0, right),
        x_copy(3, xr2, (x2_ss, x2_rs), 1, left),
        x_copy(4, xr2, (x2_ss, x2_rs), 2, right),
        x_copy(5, xr2, (x2_ss, x2_rs), 3, left),
    ]
    for k in range(2):
        core_sum(k)
        x1[k].start()
    for k in range(2, 4):
        core_sum(k)
        x2[k - 2].start()
    for k in range(4, 8):
        core_sum(k)

    def finish_dx(c, acc):
        part = slice(c * L, (c + 1) * L)
        bm, cm = bcv[part, 0:L], bcv[part, L : 2 * L]
        ys = nt(st2[c], cm)
        dxs = nt(ca2[c], bm)
        yt = y_loc[c] + rows_v[0, c : c + 1] * (ys[0:64] + ys[64:128])
        dxt = dx_loc[c] + rows_v[1, c : c + 1] * (dxs[0:64] + dxs[64:128])
        hi, lo = split2(dxt)
        xg_ref[:, part] = hi
        none = jnp.zeros((64, L), BF16)
        both = jnp.concatenate(
            [jnp.concatenate([hi, none], axis=0), jnp.concatenate([lo, none], axis=0)], axis=1
        )
        place = place_v[c]
        v = jnp.sum(dyv[:, part].astype(F32) * yt - xv[:, part].astype(F32) * dxt, axis=0, keepdims=True)
        if c < 7:
            end = with_edge(st_loc[c + 1], pre_b[c + 1], start)
        else:
            end = with_edge(st_loc[8], jnp.broadcast_to(device_decay, (8, L)), start)
        edge = jnp.sum(with_edge(ca_loc[c], suf_b[c], carry) * end, axis=0, keepdims=True)
        ve[c : c + 1, 0:L] = v
        ve[c : c + 1, L : 2 * L] = edge
        return acc + nt(jnp.concatenate([place, place], axis=1), both)

    acc = ids_v[...]
    for c in range(4):
        acc = finish_dx(c, acc)
    for k in range(2):
        x1[k].wait_recv()
        csum[4 + k] = csum[4 + k] + xr1[k]
        x2[2 + k].start()
    for c in range(4, 8):
        acc = finish_dx(c, acc)
    ns[...] = acc.reshape(nz, plan.slots, L)

    def news_copy(d):
        to = lax.rem(zi + d, nz)
        return pltpu.make_async_remote_copy(
            src_ref=ns.at[to], dst_ref=nr.at[zi], send_sem=n_ss.at[d], recv_sem=n_rs.at[zi],
            device_id=at_z(to), device_id_type=MESH,
        )

    for d in range(1, nz):
        news_copy(d).start()
    nr[zi] = ns[zi]

    parts = [p for p in split3(ve[...])]
    sums = nn(
        jnp.concatenate([*parts, jnp.zeros((8, 2 * L), F32)], axis=0).astype(BF16),
        jnp.concatenate([down, jnp.ones((L, L), BF16)], axis=0),
    )
    dla_ref[...] = sums[0:8] + sums[8:16] + sums[16:24]

    def y_copy(d):
        to = lax.rem(yi + d, ny)
        return pltpu.make_async_remote_copy(
            src_ref=ysum.at[to], dst_ref=yrecv.at[yi], send_sem=y_ss.at[d], recv_sem=y_rs.at[yi],
            device_id=at_head(head(xi, to, core)), device_id_type=MESH,
        )

    for k in range(4):
        x2[k].wait_recv()
    ysum[0 : plan.blocks] = csum[6] + xr2[2] + xr2[1]
    ysum[plan.blocks : 2 * plan.blocks] = csum[7] + xr2[0] + xr2[3]
    for d in range(1, ny):
        y_copy(d).start()
    total = ysum[yi]

    for d in range(1, nz):
        source = lax.rem(zi + nz - d, nz)
        pltpu.make_async_remote_copy(
            src_ref=ns.at[0], dst_ref=nr.at[source], send_sem=n_ss.at[d], recv_sem=n_rs.at[source],
            device_id=at_z(source), device_id_type=MESH,
        ).wait_recv()
    tiles = nr[...].reshape(ns_rows, L)
    lane = iota((ns_rows, L), 1)
    row_hit = jnp.where((lane >= 64) & (tiles == (lane - 63).astype(F32)), 1.0, 0.0).T.astype(BF16)
    hi, lo = split2(tiles)
    news_ref[...] = (nn(row_hit, hi) + nn(row_hit, lo))[64:128, 0:64]

    for d in range(1, ny):
        source = lax.rem(yi + ny - d, ny)
        pltpu.make_async_remote_copy(
            src_ref=ysum.at[0], dst_ref=yrecv.at[source], send_sem=y_ss.at[d], recv_sem=y_rs.at[source],
            device_id=twin, device_id_type=MESH,
        ).wait_recv()
        total = total + yrecv[source]
    bcg_ref[...] = total

    for d in range(1, nz):
        to, copy = dec_copy(d)
        pl.when(plan.is_owner(to))(copy.wait_send)
        to, copy = z1_copy(d)

        @pl.when(plan.is_owner(to))
        def _():
            copy.wait_send()

        news_copy(d).wait_send()

    @pl.when(plan.is_owner(zi))
    def _():
        for d in range(1, nz):
            pltpu.make_async_remote_copy(
                src_ref=zo.at[0], dst_ref=zb.at[0], send_sem=z2_ss.at[d], recv_sem=z2_rs.at[0],
                device_id=at_z(lax.rem(zi + d, nz)), device_id_type=MESH,
            ).wait_send()

    for k, c in enumerate(order):
        core_copy(c, k).wait_send()
    for copy in x1 + x2:
        copy.wait_send()
    for d in range(1, ny):
        y_copy(d).wait_send()


def on_device(plan, xs, bc, log_decay, out_grad, news_owner, news_local):
    rows = plan.tm * plan.slots
    dma = pltpu.SemaphoreType.DMA
    vm = pltpu.VMEM
    slab = (plan.blocks, plan.block, 2 * L)
    scratch = [
        vm((64, 1024), BF16), vm((64, 1024), BF16), vm((1024, 2 * L), BF16), vm((8, L), F32),
        vm((1, NQ), jnp.int32), vm((1, NQ), jnp.int32),
        vm((8, L, L), BF16), vm((8, L, L), BF16), vm((8, L, L), F32), vm((8, L, L), F32),
        vm((9, 64, L), F32), vm((8, 64, L), F32), vm((8, 8, L), F32), vm((8, 8, L), F32), vm((2, 8, L), F32),
        vm((8, L, 2 * L), F32), vm((8, plan.blocks, 2, plan.block, 2 * L), F32),
        vm((8, *slab), F32), vm((8, *slab), F32), vm((2, *slab), F32), vm((4, *slab), F32),
        vm((plan.y, plan.block, 2 * L), F32), vm((plan.y, plan.block, 2 * L), F32),
        vm((8, 64, L), F32), vm((8, 64, L), F32), vm((8, L, L), BF16), vm((8, L, L), BF16),
        vm((8, rows, L), BF16), vm((rows, L), F32), vm((8, 2 * L), F32),
        vm((1, L), F32), vm((plan.tm, 1, L), F32),
        vm((plan.owners, 2, plan.rows, L), F32), vm((plan.tm, 2, plan.rows, L), F32),
        vm((plan.tm, 2, plan.rows, L), F32), vm((plan.owners, 2, plan.rows, L), F32),
        vm((plan.tm, plan.slots, L), F32), vm((plan.tm, plan.slots, L), F32),
        dma((6,)),
        dma((plan.tm,)), dma((plan.tm,)), dma((plan.tm,)), dma((plan.tm,)), dma((plan.tm,)), dma((plan.tm,)),
        dma((8,)), dma((8,)), dma((2,)), dma((2,)), dma((4,)), dma((4,)),
        dma((plan.y,)), dma((plan.y,)), dma((plan.tm,)), dma((plan.tm,)),
    ]
    vmem = pl.BlockSpec(memory_space=pltpu.VMEM)
    anywhere = pl.BlockSpec(memory_space=pl.ANY)
    xg, bcg, dla, news = pl.pallas_call(
        functools.partial(kernel, plan),
        out_shape=(
            jax.ShapeDtypeStruct((64, 1024), BF16),
            jax.ShapeDtypeStruct((plan.block, 2 * L), F32),
            jax.ShapeDtypeStruct((8, L), F32),
            jax.ShapeDtypeStruct((NEWS_DEV, 64), F32),
        ),
        in_specs=[anywhere] * 6,
        out_specs=(vmem,) * 4,
        scratch_shapes=scratch,
        compiler_params=pltpu.CompilerParams(
            collective_id=0, has_side_effects=True, vmem_limit_bytes=40 * 2**20
        ),
    )(
        xs.T, out_grad.T, bc, log_decay.reshape(8, L), news_owner.reshape(1, NQ), news_local.reshape(1, NQ)
    )
    return xg.T, bcg, dla.reshape(1024, 1), news


def solution(mesh):
    tm, heads = mesh.shape["tm"], mesh.shape["head"]
    plan = Plan(tm, 4, heads // 8, 8 if tm == 12 else 32)
    return jax.shard_map(
        functools.partial(on_device, plan),
        mesh=mesh,
        in_specs=(
            P("tm", "head"), P("tm", None), P("tm", "head"), P("tm", "head"), P("tm", None), P("tm", None),
        ),
        out_specs=(P("tm", "head"), P(("tm", "head"), None), P("tm", "head"), P("tm", "head")),
        check_vma=False,
    )
```

```python
import functools

import jax
import jax.numpy as jnp
from jax import lax
from jax.experimental import pallas as pl
from jax.experimental.pallas import tpu as pltpu
from jax.sharding import PartitionSpec as P

MESH = pl.DeviceIdType.MESH
F32 = jnp.float32
BF16 = jnp.bfloat16
NEWS_DEV = 64
NQ = 32
L = 128


def nn(a, b):
    return lax.dot_general(a, b, (((1,), (0,)), ((), ())), preferred_element_type=F32)


def nt(a, b):
    return lax.dot_general(a, b, (((1,), (1,)), ((), ())), preferred_element_type=F32)


def split2(v):
    hi = v.astype(BF16)
    return hi, (v - hi.astype(F32)).astype(BF16)


def split3(v):
    one = v.astype(BF16).astype(F32)
    two = (v - one).astype(BF16).astype(F32)
    return one, two, v - one - two


def scaled(tiles, tile):
    return (tiles.reshape(8, 8, L) * tile[None]).reshape(64, L)


def iota(shape, dim):
    return lax.broadcasted_iota(jnp.int32, shape, dim)


class Plan:
    def __init__(self, tm, groups, x, y, slots):
        self.tm, self.groups, self.x, self.y, self.slots = tm, groups, x, y, slots
        self.size = tm // groups
        self.block = 1024 // (x * y * 2)
        self.blocks = L // (2 * self.block)
        self.chunks = 8 // x


def kernel(
    plan,
    x_hbm, dy_hbm, bc_hbm, la_hbm, own_hbm, loc_hbm,
    xg_ref, bcg_ref, dla_ref, news_ref,
    xv, dyv, bcv, lav, ownv, locv,
    xyd, col_v, st_loc, scale_v, rows_v,
    loc_bc, dbc, crecv, csum, xrecv, ysum, yrecv,
    y_loc, dx_loc, st2, place_v, ids_v, vx_v, ve,
    g_in, s_in, whole_s, whole_r, edge_v, ns, nr,
    in_sem, g_ss, g_rs, s_ss, s_rs, w_ss, w_rs,
    c_ss, c_rs, x_ss, x_rs, y_ss, y_rs, n_ss, n_rs,
):
    nz, ny, nx = plan.tm, plan.y, plan.x
    zi = lax.axis_index("tm")
    hi_ = lax.axis_index("head")
    core = lax.rem(hi_, 2)
    yi = lax.rem(hi_ // 2, ny)
    xi = hi_ // (2 * ny)

    def head(x, y, c):
        return (x * ny + y) * 2 + c

    def at_z(z):
        return (z, hi_)

    def at_head(h):
        return (zi, h)

    ng, gs = plan.groups, plan.size
    group, place_in = zi // gs, lax.rem(zi, gs)
    collects = (place_in == 0) | (place_in == gs - 1)
    twin = at_head(head(xi, yi, 1 - core))

    loads = [
        pltpu.make_async_copy(src, dst, in_sem.at[k])
        for k, (src, dst) in enumerate(
            ((la_hbm, lav), (dy_hbm, dyv), (bc_hbm, bcv), (x_hbm, xv), (own_hbm, ownv), (loc_hbm, locv))
        )
    ]
    for load in loads:
        load.start()

    barrier = pltpu.get_barrier_semaphore()
    greeted = [at_z(lax.rem(zi + d, nz)) for d in range(1, nz)]
    greeted += [twin]
    greeted += [at_head(head(lax.rem(xi + d, nx), yi, core)) for d in range(1, nx)]
    greeted += [at_head(head(xi, lax.rem(yi + d, ny), core)) for d in range(1, ny)]
    for device in greeted:
        pl.semaphore_signal(barrier, inc=1, device_id=device, device_id_type=MESH)

    up = jnp.where(iota((L, L), 0) <= iota((L, L), 1), 1.0, 0.0).astype(BF16)
    down = jnp.where(iota((L, L), 0) >= iota((L, L), 1), 1.0, 0.0).astype(BF16)
    loads[0].wait()
    parts = split3(lav[...])
    sums = nn(jnp.concatenate([*parts, jnp.zeros((8, L), F32)], axis=0).astype(BF16), up)
    cums = sums[0:8] + sums[8:16] + sums[16:24]
    tot = jnp.broadcast_to(cums[:, L - 1 : L], (8, L))
    after = jnp.exp(cums)
    before = jnp.exp(tot - cums)
    chunk_decay = jnp.exp(tot)
    tots = [tot[c : c + 1] for c in range(8)]
    run = jnp.zeros((1, L), F32)
    for c in range(8):
        scale_v[0, c] = jnp.broadcast_to(jnp.exp(run), (8, L))
        run = run + tots[c]
    device_decay = jnp.exp(run)
    run = jnp.zeros((1, L), F32)
    for c in reversed(range(8)):
        scale_v[1, c] = jnp.broadcast_to(jnp.exp(run), (8, L))
        run = run + tots[c]
    decay_tile = jnp.broadcast_to(device_decay, (8, L))

    def in_group(buf, sems, q):
        return pltpu.make_async_remote_copy(
            src_ref=buf.at[place_in], dst_ref=buf.at[place_in], send_sem=sems[0].at[q], recv_sem=sems[1].at[place_in],
            device_id=at_z(group * gs + q), device_id_type=MESH,
        )

    def arrived(buf, sems, q):
        pltpu.make_async_remote_copy(
            src_ref=buf.at[q], dst_ref=buf.at[q], send_sem=sems[0].at[q], recv_sem=sems[1].at[q],
            device_id=twin, device_id_type=MESH,
        ).wait_recv()

    g_sems, s_sems = (g_ss, g_rs), (s_ss, s_rs)

    def takes_g(q):
        return (q != place_in) & ((q < place_in) | (q == gs - 1))

    def takes_s(q):
        return (q != place_in) & ((q > place_in) | (q == 0))

    loads[1].wait()
    loads[2].wait()
    back = jnp.zeros((64, L), F32)
    for c in reversed(range(8)):
        part = slice(c * L, (c + 1) * L)
        hi, lo = split2(dyv[:, part].astype(F32) * after[c : c + 1])
        cm = bcv[part, L : 2 * L]
        st_loc[1, c] = back
        back = back * chunk_decay[c : c + 1] + nn(
            jnp.concatenate([hi, lo], axis=1), jnp.concatenate([cm, cm], axis=0)
        )
    g_in[place_in, 0:64] = back
    g_in[place_in, 64:72] = decay_tile

    pl.semaphore_wait(barrier, len(greeted))

    for q in reversed(range(gs)):

        @pl.when(takes_g(q))
        def _():
            in_group(g_in, g_sems, q).start()

    loads[3].wait()
    state = jnp.zeros((64, L), F32)
    for c in range(8):
        part = slice(c * L, (c + 1) * L)
        hi, lo = split2(xv[:, part].astype(F32) * before[c : c + 1])
        bm = bcv[part, 0:L]
        st_loc[0, c] = state
        state = state * chunk_decay[c : c + 1] + nn(
            jnp.concatenate([hi, lo], axis=1), jnp.concatenate([bm, bm], axis=0)
        )
    st_loc[0, 8] = state
    s_in[place_in, 0:64] = state
    s_in[place_in, 64:72] = decay_tile
    for q in range(gs):

        @pl.when(takes_s(q))
        def _():
            in_group(s_in, s_sems, q).start()

    big = jnp.concatenate([cums, after, before, jnp.zeros((L - 24, L), F32)], axis=0).T
    lower = iota((L, L), 0) >= iota((L, L), 1)
    upper = iota((L, L), 0) <= iota((L, L), 1)
    rows_v[0] = after
    rows_v[1] = before

    def local(c):
        part = slice(c * L, (c + 1) * L)
        bm, cm = bcv[part, 0:L], bcv[part, L : 2 * L]
        xt, dyt = xv[:, part], dyv[:, part]
        xf, dyf = xt.astype(F32), dyt.astype(F32)
        x2 = jnp.concatenate([xf, xf], axis=0).T.astype(BF16)
        dy2 = jnp.concatenate([dyf, dyf], axis=0).T.astype(BF16)
        xyd[0, c] = dy2
        xyd[1, c] = x2
        col = jnp.broadcast_to(big[:, c : c + 1], (L, L))
        col_v[0, c] = jnp.broadcast_to(big[:, 8 + c : 9 + c], (L, L))
        col_v[1, c] = jnp.broadcast_to(big[:, 16 + c : 17 + c], (L, L))
        row = jnp.broadcast_to(cums[c : c + 1], (L, L))
        m = jnp.exp(jnp.where(lower, col - row, -1e30))
        mt = jnp.exp(jnp.where(upper, row - col, -1e30))
        w = split2(m * nt(cm, bm))
        q = split2(m * nn(dy2[:, 0:64], xt))
        qt = split2(mt * nn(x2[:, 0:64], dyt))
        loc_bc[1, c] = nn(jnp.concatenate(qt, axis=1), jnp.concatenate([cm, cm], axis=0))
        loc_bc[0, c] = nn(jnp.concatenate(q, axis=1), jnp.concatenate([bm, bm], axis=0))
        y_loc[c] = nt(jnp.concatenate([xt, xt], axis=1), jnp.concatenate(w, axis=1))
        dx_loc[c] = nn(jnp.concatenate([dyt, dyt], axis=1), jnp.concatenate(w, axis=0))

    for c in range(8):
        local(c)

    def spans():
        return [(o, 2 * o <= ng) for o in range(1, ng)]

    def whole_copy(o, q):
        to = lax.rem(group + o, ng)
        kind = 1 - (group + o) // ng
        return pltpu.make_async_remote_copy(
            src_ref=whole_s.at[kind], dst_ref=whole_r.at[group], send_sem=w_ss.at[o, q], recv_sem=w_rs.at[group],
            device_id=at_z(to * gs + q), device_id_type=MESH,
        )

    def sender(up):
        return place_in == (gs - 1 if up else 0)

    @pl.when(collects)
    def _():
        for q in range(gs):

            @pl.when(q != place_in)
            def _():
                arrived(g_in, g_sems, q)

        decay = jnp.ones((8, L), F32)
        total = jnp.zeros((64, L), F32)
        for q in reversed(range(gs)):
            total = g_in[q, 0:64] + scaled(total, g_in[q, 64:72])
            decay = decay * g_in[q, 64:72]
        whole_s[0, 0:64] = total
        whole_s[0, 64:72] = decay
        whole_s[1, 64:72] = decay
        for o, up in spans():
            for q in range(gs) if up else reversed(range(gs)):

                @pl.when(sender(up) & (lax.rem(group + o, ng) < group))
                def _():
                    whole_copy(o, q).start()

        for q in range(gs):

            @pl.when(q != place_in)
            def _():
                arrived(s_in, s_sems, q)

        total = jnp.zeros((64, L), F32)
        for q in range(gs):
            total = s_in[q, 0:64] + scaled(total, s_in[q, 64:72])
        whole_s[1, 0:64] = total
        for o, up in spans():
            for q in range(gs) if up else reversed(range(gs)):

                @pl.when(sender(up) & (lax.rem(group + o, ng) > group))
                def _():
                    whole_copy(o, q).start()

    ns_rows = nz * plan.slots
    loads[4].wait()
    loads[5].wait()
    owner_row = ownv[...]
    named = jnp.where(iota((16, NQ), 0) == owner_row, 1.0, 0.0)
    earlier = jnp.where(iota((NQ, NQ), 0) < iota((NQ, NQ), 1), 1.0, 0.0)
    rank = jnp.sum(named * nn(named.astype(BF16), earlier.astype(BF16)), axis=0, keepdims=True)
    slot = owner_row.astype(F32) * plan.slots + rank
    spread = jnp.where(iota((NQ, 1024), 0) == iota((NQ, 1024), 1) // NQ, 1.0, 0.0).astype(BF16)
    slot_t = nn(jnp.broadcast_to(slot, (16, NQ)).astype(BF16), spread)
    for c in range(8):
        hit = slot_t[0:1, c * L : (c + 1) * L] == iota((ns_rows, L), 0).astype(F32)
        place_v[c] = jnp.where(hit, 1.0, 0.0).astype(BF16)
    hit = slot == iota((ns_rows, NQ), 0).astype(F32)
    ids = jnp.sum(jnp.where(hit, locv[...].astype(F32) + 1.0, 0.0), axis=1, keepdims=True)
    ids_v[...] = jnp.where(iota((ns_rows, L), 1) >= 64, ids, 0.0)

    def whole_arrived(a):
        pltpu.make_async_remote_copy(
            src_ref=whole_s.at[0], dst_ref=whole_r.at[a], send_sem=w_ss.at[0, 0], recv_sem=w_rs.at[a],
            device_id=twin, device_id_type=MESH,
        ).wait_recv()

    def state_edge():
        edge_v[0] = jnp.zeros((64, L), F32)
        for a in range(ng):

            @pl.when(a < group)
            def _():
                whole_arrived(a)
                edge_v[0] = whole_r[a, 0:64] + scaled(edge_v[0], whole_r[a, 64:72])

        for q in range(gs):

            @pl.when((q < place_in) & (place_in != gs - 1))
            def _():
                arrived(s_in, s_sems, q)

            @pl.when(q < place_in)
            def _():
                edge_v[0] = s_in[q, 0:64] + scaled(edge_v[0], s_in[q, 64:72])

    def gradient_edge():
        edge_v[1] = jnp.zeros((64, L), F32)
        for a in reversed(range(ng)):

            @pl.when(a > group)
            def _():
                whole_arrived(a)
                edge_v[1] = whole_r[a, 0:64] + scaled(edge_v[1], whole_r[a, 64:72])

        for q in reversed(range(gs)):

            @pl.when((q > place_in) & (place_in != 0))
            def _():
                arrived(g_in, g_sems, q)

            @pl.when(q > place_in)
            def _():
                edge_v[1] = g_in[q, 0:64] + scaled(edge_v[1], g_in[q, 64:72])

    def with_edge(kind, c, edge):
        return st_loc[kind, c] + scaled(edge, scale_v[kind, c])

    span = plan.chunks
    steps = [lax.rem(xi + d, nx) for d in ([2, 1, 3] if nx == 4 else range(1, nx))] + [xi]
    order = [t * span + i for t in steps for i in range(span)]

    def core_copy(kind, c, k):
        return pltpu.make_async_remote_copy(
            src_ref=dbc.at[kind, c, :, 1 - core], dst_ref=crecv.at[kind, c],
            send_sem=c_ss.at[kind, k], recv_sem=c_rs.at[kind, k], device_id=twin, device_id_type=MESH,
        )

    def x_copy(kind, to):
        return pltpu.make_async_remote_copy(
            src_ref=csum.at[kind, pl.ds(to * span, span)], dst_ref=xrecv.at[kind, xi],
            send_sem=x_ss.at[kind, to], recv_sem=x_rs.at[kind, xi],
            device_id=at_head(head(to, yi, core)), device_id_type=MESH,
        )

    def y_copy(kind, d):
        to = lax.rem(yi + d, ny)
        return pltpu.make_async_remote_copy(
            src_ref=ysum.at[kind, to], dst_ref=yrecv.at[kind, yi], send_sem=y_ss.at[kind, d], recv_sem=y_rs.at[kind, yi],
            device_id=at_head(head(xi, to, core)), device_id_type=MESH,
        )

    def over_cores_and_out(kind):
        for n, to in enumerate(steps):
            for i in range(span):
                k = n * span + i
                c = order[k]
                core_copy(kind, c, k).wait_recv()
                csum[kind, c] = dbc[kind, c, :, core] + crecv[kind, c]
            if n < nx - 1:
                x_copy(kind, to).start()

    news_order = sorted(range(1, nz), key=lambda d: -min(d, nz - d))
    y_order = sorted(range(1, ny), key=lambda d: -min(d, ny - d))

    def over_x_and_out(kind):
        total = csum[kind, pl.ds(xi * span, span)]
        for d in range(1, nx):
            source = lax.rem(xi + d, nx)
            pltpu.make_async_remote_copy(
                src_ref=xrecv.at[kind, source], dst_ref=xrecv.at[kind, source],
                send_sem=x_ss.at[kind, 0], recv_sem=x_rs.at[kind, source], device_id=twin, device_id_type=MESH,
            ).wait_recv()
            total = total + xrecv[kind, source]
        ysum[kind] = total.reshape(ny, plan.block, L)
        for d in y_order:
            y_copy(kind, d).start()

    def over_y(kind):
        total = ysum[kind, yi]
        for d in y_order:
            source = lax.rem(yi + d, ny)
            pltpu.make_async_remote_copy(
                src_ref=ysum.at[kind, 0], dst_ref=yrecv.at[kind, source],
                send_sem=y_ss.at[kind, 0], recv_sem=y_rs.at[kind, source], device_id=twin, device_id_type=MESH,
            ).wait_recv()
            total = total + yrecv[kind, source]
        bcg_ref[:, pl.ds(pl.multiple_of((1 - kind) * L, L), L)] = total

    def finish_dx(c, acc):
        part = slice(c * L, (c + 1) * L)
        dxs = nt(st2[1, c], bcv[part, 0:L])
        dxt = dx_loc[c] + rows_v[1, c : c + 1] * (dxs[0:64] + dxs[64:128])
        hi, lo = split2(dxt)
        xg_ref[:, part] = hi
        none = jnp.zeros((64, L), BF16)
        both = jnp.concatenate(
            [jnp.concatenate([hi, none], axis=0), jnp.concatenate([lo, none], axis=0)], axis=1
        )
        place = place_v[c]
        vx_v[c : c + 1] = jnp.sum(xv[:, part].astype(F32) * dxt, axis=0, keepdims=True)
        return acc + nt(jnp.concatenate([place, place], axis=1), both)

    def news_copy(d):
        to = lax.rem(zi + d, nz)
        return pltpu.make_async_remote_copy(
            src_ref=ns.at[to], dst_ref=nr.at[zi], send_sem=n_ss.at[d], recv_sem=n_rs.at[zi],
            device_id=at_z(to), device_id_type=MESH,
        )

    first = (group + 1) // ng
    shape = (plan.blocks, 2, plan.block, L)

    def phase(i, carried):
        kind = first + i - 2 * first * i
        pl.when(kind == 0)(state_edge)
        pl.when(kind == 1)(gradient_edge)
        edge = edge_v[kind]
        for k, c in enumerate(order):
            st = jnp.concatenate(split2(with_edge(kind, c, edge)), axis=0)
            st2[kind, c] = st
            dbc[kind, c] = (loc_bc[kind, c] + col_v[kind, c] * nn(xyd[kind, c], st)).reshape(shape)
            core_copy(kind, c, k).start()
        over_cores_and_out(kind)

        @pl.when(kind == 1)
        def _():
            acc = ids_v[...]
            for c in range(8):
                acc = finish_dx(c, acc)
            ns[...] = acc.reshape(nz, plan.slots, L)
            for d in news_order:
                news_copy(d).start()
            nr[zi] = ns[zi]

        return carried

    lax.fori_loop(0, 2, phase, 0)
    over_x_and_out(first)

    start, carry = edge_v[0], edge_v[1]
    for c in range(8):
        part = slice(c * L, (c + 1) * L)
        ys = nt(st2[0, c], bcv[part, L : 2 * L])
        yt = y_loc[c] + rows_v[0, c : c + 1] * (ys[0:64] + ys[64:128])
        vy = jnp.sum(dyv[:, part].astype(F32) * yt, axis=0, keepdims=True)
        if c < 7:
            end = with_edge(0, c + 1, start)
        else:
            end = st_loc[0, 8] + scaled(start, decay_tile)
        ve[c : c + 1, 0:L] = vy - vx_v[c : c + 1]
        ve[c : c + 1, L : 2 * L] = jnp.sum(with_edge(1, c, carry) * end, axis=0, keepdims=True)
    over_x_and_out(1 - first)
    parts = split3(ve[...])
    sums = nn(
        jnp.concatenate([*parts, jnp.zeros((8, 2 * L), F32)], axis=0).astype(BF16),
        jnp.concatenate([down, jnp.ones((L, L), BF16)], axis=0),
    )
    dla_ref[...] = sums[0:8] + sums[8:16] + sums[16:24]
    over_y(first)

    for d in range(1, nz):
        source = lax.rem(zi + nz - d, nz)
        pltpu.make_async_remote_copy(
            src_ref=ns.at[0], dst_ref=nr.at[source], send_sem=n_ss.at[d], recv_sem=n_rs.at[source],
            device_id=at_z(source), device_id_type=MESH,
        ).wait_recv()
    tiles = nr[...].reshape(ns_rows, L)
    lane = iota((ns_rows, L), 1)
    row_hit = jnp.where((lane >= 64) & (tiles == (lane - 63).astype(F32)), 1.0, 0.0).T.astype(BF16)
    hi, lo = split2(tiles)
    news_ref[...] = (nn(row_hit, hi) + nn(row_hit, lo))[64:128, 0:64]

    over_y(1 - first)

    for q in range(gs):

        @pl.when(takes_g(q))
        def _():
            in_group(g_in, g_sems, q).wait_send()

        @pl.when(takes_s(q))
        def _():
            in_group(s_in, s_sems, q).wait_send()

        for o, up in spans():

            @pl.when(sender(up))
            def _():
                whole_copy(o, q).wait_send()

    for d in range(1, nz):
        news_copy(d).wait_send()
    for kind in range(2):
        for k, c in enumerate(order):
            core_copy(kind, c, k).wait_send()
        for to in steps[:-1]:
            x_copy(kind, to).wait_send()
        for d in range(1, ny):
            y_copy(kind, d).wait_send()


def on_device(plan, xs, bc, log_decay, out_grad, news_owner, news_local):
    rows = plan.tm * plan.slots
    dma = pltpu.SemaphoreType.DMA
    vm = pltpu.VMEM
    shapes = (
        jax.ShapeDtypeStruct((64, 1024), BF16),
        jax.ShapeDtypeStruct((plan.block, 2 * L), F32),
        jax.ShapeDtypeStruct((8, L), F32),
        jax.ShapeDtypeStruct((NEWS_DEV, 64), F32),
    )
    slab = (plan.blocks, plan.block, L)
    ng, gs, nx, ny = plan.groups, plan.size, plan.x, plan.y
    scratch = [
        vm((64, 1024), BF16), vm((64, 1024), BF16), vm((1024, 2 * L), BF16), vm((8, L), F32),
        vm((1, NQ), jnp.int32), vm((1, NQ), jnp.int32),
        vm((2, 8, L, L), BF16), vm((2, 8, L, L), F32), vm((2, 9, 64, L), F32), vm((2, 8, 8, L), F32), vm((2, 8, L), F32),
        vm((2, 8, L, L), F32), vm((2, 8, plan.blocks, 2, plan.block, L), F32),
        vm((2, 8, *slab), F32), vm((2, 8, *slab), F32), vm((2, nx, plan.chunks, *slab), F32),
        vm((2, ny, plan.block, L), F32), vm((2, ny, plan.block, L), F32),
        vm((8, 64, L), F32), vm((8, 64, L), F32), vm((2, 8, L, L), BF16),
        vm((8, rows, L), BF16), vm((rows, L), F32), vm((8, L), F32), vm((8, 2 * L), F32),
        vm((gs, 72, L), F32), vm((gs, 72, L), F32), vm((2, 72, L), F32), vm((ng, 72, L), F32), vm((2, 64, L), F32),
        vm((plan.tm, plan.slots, L), F32), vm((plan.tm, plan.slots, L), F32),
        dma((6,)),
        dma((gs,)), dma((gs,)), dma((gs,)), dma((gs,)), dma((ng, gs)), dma((ng,)),
        dma((2, 8)), dma((2, 8)), dma((2, nx)), dma((2, nx)), dma((2, ny)), dma((2, ny)),
        dma((plan.tm,)), dma((plan.tm,)),
    ]
    anywhere = pl.BlockSpec(memory_space=pl.ANY)
    xg, bcg, dla, news = pl.pallas_call(
        functools.partial(kernel, plan),
        out_shape=shapes,
        in_specs=[anywhere] * 6,
        out_specs=(pl.BlockSpec(memory_space=pltpu.VMEM),) * 4,
        scratch_shapes=scratch,
        compiler_params=pltpu.CompilerParams(
            collective_id=0, has_side_effects=True, vmem_limit_bytes=55000 * 1024
        ),
    )(
        xs.T, out_grad.T, bc, log_decay.reshape(8, L), news_owner.reshape(1, NQ), news_local.reshape(1, NQ)
    )
    return xg.T, bcg, dla.reshape(1024, 1), news


def solution(mesh):
    tm, heads = mesh.shape["tm"], mesh.shape["head"]
    plan = Plan(tm, 3, 4, heads // 8, 8 if tm == 12 else 32)
    return jax.shard_map(
        functools.partial(on_device, plan),
        mesh=mesh,
        in_specs=(
            P("tm", "head"), P("tm", None), P("tm", "head"), P("tm", "head"), P("tm", None), P("tm", None),
        ),
        out_specs=(P("tm", "head"), P(("tm", "head"), None), P("tm", "head"), P("tm", "head")),
        check_vma=False,
    )
```

```python
import functools

import jax
import jax.numpy as jnp
from jax import lax
from jax.experimental import pallas as pl
from jax.experimental.pallas import tpu as pltpu
from jax.sharding import PartitionSpec as P

MESH = pl.DeviceIdType.MESH
F32 = jnp.float32
BF16 = jnp.bfloat16
NEWS_DEV = 64
NQ = 32
L = 128


def nn(a, b):
    return lax.dot_general(a, b, (((1,), (0,)), ((), ())), preferred_element_type=F32)


def nt(a, b):
    return lax.dot_general(a, b, (((1,), (1,)), ((), ())), preferred_element_type=F32)


def split2(v):
    hi = v.astype(BF16)
    return hi, (v - hi.astype(F32)).astype(BF16)


def split3(v):
    one = v.astype(BF16).astype(F32)
    two = (v - one).astype(BF16).astype(F32)
    return one, two, v - one - two


def scaled(tiles, tile):
    return (tiles.reshape(8, 8, L) * tile[None]).reshape(64, L)


def iota(shape, dim):
    return lax.broadcasted_iota(jnp.int32, shape, dim)


class Plan:
    def __init__(self, tm, groups, x, y, slots):
        self.tm, self.groups, self.x, self.y, self.slots = tm, groups, x, y, slots
        self.size = tm // groups
        self.block = 1024 // (x * y * 2)
        self.blocks = L // (2 * self.block)
        self.chunks = 8 // x


def kernel(
    plan,
    x_hbm, dy_hbm, bc_hbm, la_hbm, own_hbm, loc_hbm,
    xg_ref, bcg_ref, dla_ref, news_ref,
    xv, dyv, bcv, lav, ownv, locv,
    xyd, col_v, st_loc, scale_v, rows_v,
    loc_bc, dbc, crecv, csum, xrecv, ysum, yrecv,
    y_loc, dx_loc, st2, place_v, ids_v, vx_v, ve,
    g_in, s_in, whole_s, whole_r, edge_v, ns, nr,
    ready_g, ready_w, ready_p, in_sem, g_ss, g_rs, s_ss, s_rs, w_ss, w_rs,
    c_ss, c_rs, x_ss, x_rs, y_ss, y_rs, n_ss, n_rs,
):
    nz, ny, nx = plan.tm, plan.y, plan.x
    zi = lax.axis_index("tm")
    hi_ = lax.axis_index("head")
    core = lax.rem(hi_, 2)
    yi = lax.rem(hi_ // 2, ny)
    xi = hi_ // (2 * ny)

    def head(x, y, c):
        return (x * ny + y) * 2 + c

    def at_z(z):
        return (z, hi_)

    def at_head(h):
        return (zi, h)

    ng, gs = plan.groups, plan.size
    group, place_in = zi // gs, lax.rem(zi, gs)
    twin = at_head(head(xi, yi, 1 - core))

    loads = [
        pltpu.make_async_copy(src, dst, in_sem.at[k])
        for k, (src, dst) in enumerate(
            ((la_hbm, lav), (dy_hbm, dyv), (bc_hbm, bcv), (x_hbm, xv), (own_hbm, ownv), (loc_hbm, locv))
        )
    ]
    for load in loads:
        load.start()

    barrier = pltpu.get_barrier_semaphore()
    low, high = zi == 0, group == ng - 1
    bottom, top = place_in == 0, place_in == gs - 1

    def rank(y):
        return y + y // (ny // 2) * (ny + ny // 2 - 1 - 2 * y)

    def signal(sem, device, when):
        @pl.when(when)
        def _():
            pl.semaphore_signal(sem, inc=1, device_id=device, device_id_type=MESH)

    pairs = [(twin, core == 1)]
    for d in range(1, nx):
        to = lax.rem(xi + d, nx)
        pairs.append((at_head(head(to, yi, core)), to > xi))
    for d in range(1, ny):
        to = lax.rem(yi + d, ny)
        pairs.append((at_head(head(xi, to, core)), rank(to) > rank(yi)))

    for q in range(gs):
        signal(barrier, at_z(group * gs + q), q > place_in)
    above = lax.rem(group + 1, ng) * gs
    below = lax.rem(group + ng - 1, ng) * gs
    signal(barrier, at_z(above), group + 1 < ng - 1)
    for q in range(gs):
        signal(barrier, at_z(above + q), top & (group + 1 < ng - 1))
        signal(barrier, at_z(nz - gs + q), group < ng - 1)
    for device, later in pairs:
        signal(barrier, device, later)

    def await_count(sem, count):
        @pl.when(count > 0)
        def _():
            pl.semaphore_wait(sem, count)

    def flag(value):
        return jnp.where(value, 1, 0)

    earlier_plane = (1 - core) + xi + rank(yi)
    later_plane = nx + ny - 1 - earlier_plane
    greetings = (
        place_in + earlier_plane + flag(high) * (nz - gs)
        + flag((group > 0) & (group < ng - 1)) * (1 + gs * flag(bottom))
    )

    up = jnp.where(iota((L, L), 0) <= iota((L, L), 1), 1.0, 0.0).astype(BF16)
    down = jnp.where(iota((L, L), 0) >= iota((L, L), 1), 1.0, 0.0).astype(BF16)
    loads[0].wait()
    parts = split3(lav[...])
    sums = nn(jnp.concatenate([*parts, jnp.zeros((8, L), F32)], axis=0).astype(BF16), up)
    cums = sums[0:8] + sums[8:16] + sums[16:24]
    tot = jnp.broadcast_to(cums[:, L - 1 : L], (8, L))
    after = jnp.exp(cums)
    before = jnp.exp(tot - cums)
    chunk_decay = jnp.exp(tot)
    tots = [tot[c : c + 1] for c in range(8)]
    run = jnp.zeros((1, L), F32)
    for c in range(8):
        scale_v[0, c] = jnp.broadcast_to(jnp.exp(run), (8, L))
        run = run + tots[c]
    device_decay = jnp.exp(run)
    run = jnp.zeros((1, L), F32)
    for c in reversed(range(8)):
        scale_v[1, c] = jnp.broadcast_to(jnp.exp(run), (8, L))
        run = run + tots[c]
    decay_tile = jnp.broadcast_to(device_decay, (8, L))

    def in_group(buf, sems, q):
        return pltpu.make_async_remote_copy(
            src_ref=buf.at[place_in], dst_ref=buf.at[place_in], send_sem=sems[0].at[q], recv_sem=sems[1].at[place_in],
            device_id=at_z(group * gs + q), device_id_type=MESH,
        )

    def arrived(buf, sems, q):
        pltpu.make_async_remote_copy(
            src_ref=buf.at[q], dst_ref=buf.at[q], send_sem=sems[0].at[q], recv_sem=sems[1].at[q],
            device_id=twin, device_id_type=MESH,
        ).wait_recv()

    g_sems, s_sems = (g_ss, g_rs), (s_ss, s_rs)

    def takes_g(q):
        return (q < place_in) | ((q == gs - 1) & high & (q != place_in))

    def takes_s(q):
        return (q > place_in) | ((q == 0) & (group == 0) & (q != place_in))

    loads[1].wait()
    loads[2].wait()
    back = jnp.zeros((64, L), F32)
    for c in reversed(range(8)):
        part = slice(c * L, (c + 1) * L)
        hi, lo = split2(dyv[:, part].astype(F32) * after[c : c + 1])
        cm = bcv[part, L : 2 * L]
        st_loc[1, c] = back
        back = back * chunk_decay[c : c + 1] + nn(
            jnp.concatenate([hi, lo], axis=1), jnp.concatenate([cm, cm], axis=0)
        )
    g_in[place_in, 0:64] = back
    g_in[place_in, 64:72] = decay_tile

    await_count(barrier, greetings)
    for q in range(gs):
        signal(ready_g, at_z(group * gs + q), q < place_in)
    signal(ready_w, at_z(below + gs - 1), group > 0)
    signal(ready_w, at_z(0), high)
    for device, later in pairs:
        signal(ready_p, device, jnp.logical_not(later))

    for q in range(gs):

        @pl.when(takes_g(q) & (q < place_in))
        def _():
            in_group(g_in, g_sems, q).start()

    loads[3].wait()
    state = jnp.zeros((64, L), F32)
    for c in range(8):
        part = slice(c * L, (c + 1) * L)
        hi, lo = split2(xv[:, part].astype(F32) * before[c : c + 1])
        bm = bcv[part, 0:L]
        st_loc[0, c] = state
        state = state * chunk_decay[c : c + 1] + nn(
            jnp.concatenate([hi, lo], axis=1), jnp.concatenate([bm, bm], axis=0)
        )
    st_loc[0, 8] = state
    s_in[place_in, 0:64] = state
    s_in[place_in, 64:72] = decay_tile

    @pl.when(takes_s(0))
    def _():
        in_group(s_in, s_sems, 0).start()

    await_count(ready_g, gs - 1 - place_in)

    @pl.when(takes_g(gs - 1))
    def _():
        in_group(g_in, g_sems, gs - 1).start()

    for q in range(1, gs):

        @pl.when(takes_s(q))
        def _():
            in_group(s_in, s_sems, q).start()

    def spans():
        return [(o, 2 * o <= ng) for o in range(1, ng)]

    def whole_copy(o, q):
        to = lax.rem(group + o, ng)
        kind = 1 - (group + o) // ng
        return pltpu.make_async_remote_copy(
            src_ref=whole_s.at[kind], dst_ref=whole_r.at[group], send_sem=w_ss.at[o, q], recv_sem=w_rs.at[group],
            device_id=at_z(to * gs + q), device_id_type=MESH,
        )

    def sender(up):
        return place_in == (gs - 1 if up else 0)

    collects_g = (bottom & (group > 0)) | (zi == nz - 1)
    collects_s = low | (top & (group < ng - 1))

    @pl.when(collects_g)
    def _():
        for q in range(gs):

            @pl.when(q != place_in)
            def _():
                arrived(g_in, g_sems, q)

        decay = jnp.ones((8, L), F32)
        total = jnp.zeros((64, L), F32)
        for q in reversed(range(gs)):
            total = g_in[q, 0:64] + scaled(total, g_in[q, 64:72])
            decay = decay * g_in[q, 64:72]
        whole_s[0, 0:64] = total
        whole_s[0, 64:72] = decay
        for o, up in spans():
            for q in range(gs):

                @pl.when(sender(up) & (lax.rem(group + o, ng) < group))
                def _():
                    whole_copy(o, q).start()

    big = jnp.concatenate([cums, after, before, jnp.zeros((L - 24, L), F32)], axis=0).T
    lower = iota((L, L), 0) >= iota((L, L), 1)
    upper = iota((L, L), 0) <= iota((L, L), 1)
    rows_v[0] = after
    rows_v[1] = before

    def local(c):
        part = slice(c * L, (c + 1) * L)
        bm, cm = bcv[part, 0:L], bcv[part, L : 2 * L]
        xt, dyt = xv[:, part], dyv[:, part]
        xf, dyf = xt.astype(F32), dyt.astype(F32)
        x2 = jnp.concatenate([xf, xf], axis=0).T.astype(BF16)
        dy2 = jnp.concatenate([dyf, dyf], axis=0).T.astype(BF16)
        xyd[0, c] = dy2
        xyd[1, c] = x2
        col = jnp.broadcast_to(big[:, c : c + 1], (L, L))
        col_v[0, c] = jnp.broadcast_to(big[:, 8 + c : 9 + c], (L, L))
        col_v[1, c] = jnp.broadcast_to(big[:, 16 + c : 17 + c], (L, L))
        row = jnp.broadcast_to(cums[c : c + 1], (L, L))
        m = jnp.exp(jnp.where(lower, col - row, -1e30))
        mt = jnp.exp(jnp.where(upper, row - col, -1e30))
        w = split2(m * nt(cm, bm))
        q = split2(m * nn(dy2[:, 0:64], xt))
        qt = split2(mt * nn(x2[:, 0:64], dyt))
        loc_bc[1, c] = nn(jnp.concatenate(qt, axis=1), jnp.concatenate([cm, cm], axis=0))
        loc_bc[0, c] = nn(jnp.concatenate(q, axis=1), jnp.concatenate([bm, bm], axis=0))
        y_loc[c] = nt(jnp.concatenate([xt, xt], axis=1), jnp.concatenate(w, axis=1))
        dx_loc[c] = nn(jnp.concatenate([dyt, dyt], axis=1), jnp.concatenate(w, axis=0))

    for c in range(8):
        local(c)

    @pl.when(collects_s)
    def _():
        for q in range(gs):

            @pl.when(q != place_in)
            def _():
                arrived(s_in, s_sems, q)

        decay = jnp.ones((8, L), F32)
        total = jnp.zeros((64, L), F32)
        for q in range(gs):
            total = s_in[q, 0:64] + scaled(total, s_in[q, 64:72])
            decay = decay * s_in[q, 64:72]
        whole_s[1, 0:64] = total
        whole_s[1, 64:72] = decay
        await_count(ready_w, gs * flag(top) + gs * flag(low))
        for o, up in spans():
            for q in range(gs):

                @pl.when(sender(up) & (lax.rem(group + o, ng) > group))
                def _():
                    whole_copy(o, q).start()

    ns_rows = nz * plan.slots
    loads[4].wait()
    loads[5].wait()
    owner_row = ownv[...]
    named = jnp.where(iota((16, NQ), 0) == owner_row, 1.0, 0.0)
    earlier = jnp.where(iota((NQ, NQ), 0) < iota((NQ, NQ), 1), 1.0, 0.0)
    rank = jnp.sum(named * nn(named.astype(BF16), earlier.astype(BF16)), axis=0, keepdims=True)
    slot = owner_row.astype(F32) * plan.slots + rank
    spread = jnp.where(iota((NQ, 1024), 0) == iota((NQ, 1024), 1) // NQ, 1.0, 0.0).astype(BF16)
    slot_t = nn(jnp.broadcast_to(slot, (16, NQ)).astype(BF16), spread)
    for c in range(8):
        hit = slot_t[0:1, c * L : (c + 1) * L] == iota((ns_rows, L), 0).astype(F32)
        place_v[c] = jnp.where(hit, 1.0, 0.0).astype(BF16)
    hit = slot == iota((ns_rows, NQ), 0).astype(F32)
    ids = jnp.sum(jnp.where(hit, locv[...].astype(F32) + 1.0, 0.0), axis=1, keepdims=True)
    ids_v[...] = jnp.where(iota((ns_rows, L), 1) >= 64, ids, 0.0)

    def whole_arrived(a):
        pltpu.make_async_remote_copy(
            src_ref=whole_s.at[0], dst_ref=whole_r.at[a], send_sem=w_ss.at[0, 0], recv_sem=w_rs.at[a],
            device_id=twin, device_id_type=MESH,
        ).wait_recv()

    def state_edge():
        edge_v[0] = jnp.zeros((64, L), F32)
        for a in range(ng):

            @pl.when(a < group)
            def _():
                whole_arrived(a)
                edge_v[0] = whole_r[a, 0:64] + scaled(edge_v[0], whole_r[a, 64:72])

        for q in range(gs):

            @pl.when((q < place_in) & jnp.logical_not(collects_s))
            def _():
                arrived(s_in, s_sems, q)

            @pl.when(q < place_in)
            def _():
                edge_v[0] = s_in[q, 0:64] + scaled(edge_v[0], s_in[q, 64:72])

    def gradient_edge():
        edge_v[1] = jnp.zeros((64, L), F32)
        for a in reversed(range(ng)):

            @pl.when(a > group)
            def _():
                whole_arrived(a)
                edge_v[1] = whole_r[a, 0:64] + scaled(edge_v[1], whole_r[a, 64:72])

        for q in reversed(range(gs)):

            @pl.when((q > place_in) & jnp.logical_not(collects_g))
            def _():
                arrived(g_in, g_sems, q)

            @pl.when(q > place_in)
            def _():
                edge_v[1] = g_in[q, 0:64] + scaled(edge_v[1], g_in[q, 64:72])

    def with_edge(kind, c, edge):
        return st_loc[kind, c] + scaled(edge, scale_v[kind, c])

    span = plan.chunks
    steps = [lax.rem(xi + d, nx) for d in ([2, 1, 3] if nx == 4 else range(1, nx))] + [xi]
    order = [t * span + i for t in steps for i in range(span)]

    def core_copy(kind, c, k):
        return pltpu.make_async_remote_copy(
            src_ref=dbc.at[kind, c, :, 1 - core], dst_ref=crecv.at[kind, c],
            send_sem=c_ss.at[kind, k], recv_sem=c_rs.at[kind, k], device_id=twin, device_id_type=MESH,
        )

    def x_copy(kind, to):
        return pltpu.make_async_remote_copy(
            src_ref=csum.at[kind, pl.ds(to * span, span)], dst_ref=xrecv.at[kind, xi],
            send_sem=x_ss.at[kind, to], recv_sem=x_rs.at[kind, xi],
            device_id=at_head(head(to, yi, core)), device_id_type=MESH,
        )

    def y_copy(kind, d):
        to = lax.rem(yi + d, ny)
        return pltpu.make_async_remote_copy(
            src_ref=ysum.at[kind, to], dst_ref=yrecv.at[kind, yi], send_sem=y_ss.at[kind, d], recv_sem=y_rs.at[kind, yi],
            device_id=at_head(head(xi, to, core)), device_id_type=MESH,
        )

    def over_cores_and_out(kind):
        for n, to in enumerate(steps):
            for i in range(span):
                k = n * span + i
                c = order[k]
                core_copy(kind, c, k).wait_recv()
                csum[kind, c] = dbc[kind, c, :, core] + crecv[kind, c]
            if n < nx - 1:
                x_copy(kind, to).start()

    news_order = sorted(range(1, nz), key=lambda d: -min(d, nz - d))
    y_order = sorted(range(1, ny), key=lambda d: -min(d, ny - d))

    def over_x_and_out(kind):
        total = csum[kind, pl.ds(xi * span, span)]
        for d in range(1, nx):
            source = lax.rem(xi + d, nx)
            pltpu.make_async_remote_copy(
                src_ref=xrecv.at[kind, source], dst_ref=xrecv.at[kind, source],
                send_sem=x_ss.at[kind, 0], recv_sem=x_rs.at[kind, source], device_id=twin, device_id_type=MESH,
            ).wait_recv()
            total = total + xrecv[kind, source]
        ysum[kind] = total.reshape(ny, plan.block, L)
        for d in y_order:
            y_copy(kind, d).start()

    def over_y(kind):
        total = ysum[kind, yi]
        for d in y_order:
            source = lax.rem(yi + d, ny)
            pltpu.make_async_remote_copy(
                src_ref=ysum.at[kind, 0], dst_ref=yrecv.at[kind, source],
                send_sem=y_ss.at[kind, 0], recv_sem=y_rs.at[kind, source], device_id=twin, device_id_type=MESH,
            ).wait_recv()
            total = total + yrecv[kind, source]
        bcg_ref[:, pl.ds(pl.multiple_of((1 - kind) * L, L), L)] = total

    def finish_dx(c, acc):
        part = slice(c * L, (c + 1) * L)
        dxs = nt(st2[1, c], bcv[part, 0:L])
        dxt = dx_loc[c] + rows_v[1, c : c + 1] * (dxs[0:64] + dxs[64:128])
        hi, lo = split2(dxt)
        xg_ref[:, part] = hi
        none = jnp.zeros((64, L), BF16)
        both = jnp.concatenate(
            [jnp.concatenate([hi, none], axis=0), jnp.concatenate([lo, none], axis=0)], axis=1
        )
        place = place_v[c]
        vx_v[c : c + 1] = jnp.sum(xv[:, part].astype(F32) * dxt, axis=0, keepdims=True)
        return acc + nt(jnp.concatenate([place, place], axis=1), both)

    def news_copy(d):
        to = lax.rem(zi + d, nz)
        return pltpu.make_async_remote_copy(
            src_ref=ns.at[to], dst_ref=nr.at[zi], send_sem=n_ss.at[d], recv_sem=n_rs.at[zi],
            device_id=at_z(to), device_id_type=MESH,
        )

    await_count(ready_p, later_plane)
    first = (group + 1) // ng
    shape = (plan.blocks, 2, plan.block, L)

    def phase(i, carried):
        kind = first + i - 2 * first * i
        pl.when(kind == 0)(state_edge)
        pl.when(kind == 1)(gradient_edge)
        edge = edge_v[kind]
        for k, c in enumerate(order):
            st = jnp.concatenate(split2(with_edge(kind, c, edge)), axis=0)
            st2[kind, c] = st
            dbc[kind, c] = (loc_bc[kind, c] + col_v[kind, c] * nn(xyd[kind, c], st)).reshape(shape)
            core_copy(kind, c, k).start()
        @pl.when(kind == 1)
        def _():
            acc = ids_v[...]
            for c in range(8):
                acc = finish_dx(c, acc)
            ns[...] = acc.reshape(nz, plan.slots, L)
            for d in news_order:
                news_copy(d).start()
            nr[zi] = ns[zi]

        over_cores_and_out(kind)
        over_x_and_out(kind)
        return carried

    lax.fori_loop(0, 2, phase, 0)

    start, carry = edge_v[0], edge_v[1]
    for c in range(8):
        part = slice(c * L, (c + 1) * L)
        ys = nt(st2[0, c], bcv[part, L : 2 * L])
        yt = y_loc[c] + rows_v[0, c : c + 1] * (ys[0:64] + ys[64:128])
        vy = jnp.sum(dyv[:, part].astype(F32) * yt, axis=0, keepdims=True)
        if c < 7:
            end = with_edge(0, c + 1, start)
        else:
            end = st_loc[0, 8] + scaled(start, decay_tile)
        ve[c : c + 1, 0:L] = vy - vx_v[c : c + 1]
        ve[c : c + 1, L : 2 * L] = jnp.sum(with_edge(1, c, carry) * end, axis=0, keepdims=True)
    parts = split3(ve[...])
    sums = nn(
        jnp.concatenate([*parts, jnp.zeros((8, 2 * L), F32)], axis=0).astype(BF16),
        jnp.concatenate([down, jnp.ones((L, L), BF16)], axis=0),
    )
    dla_ref[...] = sums[0:8] + sums[8:16] + sums[16:24]
    over_y(first)

    for d in range(1, nz):
        source = lax.rem(zi + nz - d, nz)
        pltpu.make_async_remote_copy(
            src_ref=ns.at[0], dst_ref=nr.at[source], send_sem=n_ss.at[d], recv_sem=n_rs.at[source],
            device_id=at_z(source), device_id_type=MESH,
        ).wait_recv()
    tiles = nr[...].reshape(ns_rows, L)
    lane = iota((ns_rows, L), 1)
    row_hit = jnp.where((lane >= 64) & (tiles == (lane - 63).astype(F32)), 1.0, 0.0).T.astype(BF16)
    hi, lo = split2(tiles)
    news_ref[...] = (nn(row_hit, hi) + nn(row_hit, lo))[64:128, 0:64]

    over_y(1 - first)

    for q in range(gs):

        @pl.when(takes_g(q))
        def _():
            in_group(g_in, g_sems, q).wait_send()

        @pl.when(takes_s(q))
        def _():
            in_group(s_in, s_sems, q).wait_send()

        for o, up in spans():

            @pl.when(sender(up))
            def _():
                whole_copy(o, q).wait_send()

    for d in range(1, nz):
        news_copy(d).wait_send()
    for kind in range(2):
        for k, c in enumerate(order):
            core_copy(kind, c, k).wait_send()
        for to in steps[:-1]:
            x_copy(kind, to).wait_send()
        for d in range(1, ny):
            y_copy(kind, d).wait_send()


def on_device(plan, xs, bc, log_decay, out_grad, news_owner, news_local):
    rows = plan.tm * plan.slots
    dma = pltpu.SemaphoreType.DMA
    vm = pltpu.VMEM
    shapes = (
        jax.ShapeDtypeStruct((64, 1024), BF16),
        jax.ShapeDtypeStruct((plan.block, 2 * L), F32),
        jax.ShapeDtypeStruct((8, L), F32),
        jax.ShapeDtypeStruct((NEWS_DEV, 64), F32),
    )
    slab = (plan.blocks, plan.block, L)
    ng, gs, nx, ny = plan.groups, plan.size, plan.x, plan.y
    scratch = [
        vm((64, 1024), BF16), vm((64, 1024), BF16), vm((1024, 2 * L), BF16), vm((8, L), F32),
        vm((1, NQ), jnp.int32), vm((1, NQ), jnp.int32),
        vm((2, 8, L, L), BF16), vm((2, 8, L, L), F32), vm((2, 9, 64, L), F32), vm((2, 8, 8, L), F32), vm((2, 8, L), F32),
        vm((2, 8, L, L), F32), vm((2, 8, plan.blocks, 2, plan.block, L), F32),
        vm((2, 8, *slab), F32), vm((2, 8, *slab), F32), vm((2, nx, plan.chunks, *slab), F32),
        vm((2, ny, plan.block, L), F32), vm((2, ny, plan.block, L), F32),
        vm((8, 64, L), F32), vm((8, 64, L), F32), vm((2, 8, L, L), BF16),
        vm((8, rows, L), BF16), vm((rows, L), F32), vm((8, L), F32), vm((8, 2 * L), F32),
        vm((gs, 72, L), F32), vm((gs, 72, L), F32), vm((2, 72, L), F32), vm((ng, 72, L), F32), vm((2, 64, L), F32),
        vm((plan.tm, plan.slots, L), F32), vm((plan.tm, plan.slots, L), F32),
        *[pltpu.SemaphoreType.REGULAR] * 3, dma((6,)),
        dma((gs,)), dma((gs,)), dma((gs,)), dma((gs,)), dma((ng, gs)), dma((ng,)),
        dma((2, 8)), dma((2, 8)), dma((2, nx)), dma((2, nx)), dma((2, ny)), dma((2, ny)),
        dma((plan.tm,)), dma((plan.tm,)),
    ]
    anywhere = pl.BlockSpec(memory_space=pl.ANY)
    xg, bcg, dla, news = pl.pallas_call(
        functools.partial(kernel, plan),
        out_shape=shapes,
        in_specs=[anywhere] * 6,
        out_specs=(pl.BlockSpec(memory_space=pltpu.VMEM),) * 4,
        scratch_shapes=scratch,
        compiler_params=pltpu.CompilerParams(
            collective_id=0, has_side_effects=True, vmem_limit_bytes=55000 * 1024
        ),
    )(
        xs.T, out_grad.T, bc, log_decay.reshape(8, L), news_owner.reshape(1, NQ), news_local.reshape(1, NQ)
    )
    return xg.T, bcg, dla.reshape(1024, 1), news


def solution(mesh):
    tm, heads = mesh.shape["tm"], mesh.shape["head"]
    plan = Plan(tm, 3, 4, heads // 8, 8 if tm == 12 else 32)
    return jax.shard_map(
        functools.partial(on_device, plan),
        mesh=mesh,
        in_specs=(
            P("tm", "head"), P("tm", None), P("tm", "head"), P("tm", "head"), P("tm", None), P("tm", None),
        ),
        out_specs=(P("tm", "head"), P(("tm", "head"), None), P("tm", "head"), P("tm", "head")),
        check_vma=False,
    )
```

```python
import functools

import jax
import jax.numpy as jnp
from jax import lax
from jax.experimental import pallas as pl
from jax.experimental.pallas import tpu as pltpu
from jax.sharding import PartitionSpec as P

MESH = pl.DeviceIdType.MESH
F32 = jnp.float32
BF16 = jnp.bfloat16
NEWS_DEV = 64
NQ = 32
L = 128


def nn(a, b):
    return lax.dot_general(a, b, (((1,), (0,)), ((), ())), preferred_element_type=F32)


def nt(a, b):
    return lax.dot_general(a, b, (((1,), (1,)), ((), ())), preferred_element_type=F32)


def split2(v):
    hi = v.astype(BF16)
    return hi, (v - hi.astype(F32)).astype(BF16)


def split3(v):
    one = v.astype(BF16).astype(F32)
    two = (v - one).astype(BF16).astype(F32)
    return one, two, v - one - two


def scaled(tiles, tile):
    return (tiles.reshape(8, 8, L) * tile[None]).reshape(64, L)


def iota(shape, dim):
    return lax.broadcasted_iota(jnp.int32, shape, dim)


class Plan:
    def __init__(self, tm, groups, x, y, slots):
        self.tm, self.groups, self.x, self.y, self.slots = tm, groups, x, y, slots
        self.size = tm // groups
        self.block = 1024 // (x * y * 2)
        self.blocks = L // (2 * self.block)
        self.chunks = 8 // x


def kernel(
    plan,
    x_hbm, dy_hbm, bc_hbm, lav, ownv, locv,
    xg_ref, bcg_ref, dla_ref, news_ref,
    xv, dyv, bcv,
    xyd, col_v, st_loc, scale_v, rows_v,
    loc_bc, dbc, crecv, csum, xrecv, ysum, yrecv,
    y_loc, dx_loc, st2, place_v, ids_v, vx_v, ve,
    g_in, s_in, whole_s, whole_r, edge_v, ns, nr,
    ready_g, ready_w, ready_p, in_sem, g_ss, g_rs, s_ss, s_rs, w_ss, w_rs,
    c_ss, c_rs, x_ss, x_rs, y_ss, y_rs, n_ss, n_rs,
):
    nz, ny, nx = plan.tm, plan.y, plan.x
    zi = lax.axis_index("tm")
    hi_ = lax.axis_index("head")
    core = lax.rem(hi_, 2)
    yi = lax.rem(hi_ // 2, ny)
    xi = hi_ // (2 * ny)

    def head(x, y, c):
        return (x * ny + y) * 2 + c

    def at_z(z):
        return (z, hi_)

    def at_head(h):
        return (zi, h)

    ng, gs = plan.groups, plan.size
    group, place_in = zi // gs, lax.rem(zi, gs)
    twin = at_head(head(xi, yi, 1 - core))

    loads = [
        pltpu.make_async_copy(src, dst, in_sem.at[k])
        for k, (src, dst) in enumerate(
            ((dy_hbm, dyv), (bc_hbm, bcv), (x_hbm, xv))
        )
    ]
    for load in loads:
        load.start()

    barrier = pltpu.get_barrier_semaphore()
    low, high = zi == 0, group == ng - 1
    wraps = group >= ng - ng // 2
    bottom, top = place_in == 0, place_in == gs - 1

    def rank(y):
        return y + y // (ny // 2) * (ny + ny // 2 - 1 - 2 * y)

    def signal(sem, device, when):
        @pl.when(when)
        def _():
            pl.semaphore_signal(sem, inc=1, device_id=device, device_id_type=MESH)

    pairs = [(twin, core == 1)]
    for d in range(1, nx):
        to = lax.rem(xi + d, nx)
        pairs.append((at_head(head(to, yi, core)), to > xi))
    for d in range(1, ny):
        to = lax.rem(yi + d, ny)
        pairs.append((at_head(head(xi, to, core)), rank(to) > rank(yi)))

    for q in range(gs):
        signal(barrier, at_z(group * gs + q), q > place_in)
    above = lax.rem(group + 1, ng) * gs
    below = lax.rem(group + ng - 1, ng) * gs
    signal(barrier, at_z(above), group + 1 < ng - 1)
    for q in range(gs):
        signal(barrier, at_z(above + q), top & (group + 1 < ng - 1))
        signal(barrier, at_z(nz - gs + q), group < ng - 1)
    if ng == 4:
        signal(barrier, at_z(3 * gs - 1), group == 0)
        for q in range(gs):
            signal(barrier, at_z(2 * gs + q), top & (group == 0))
    for device, later in pairs:
        signal(barrier, device, later)

    def await_count(sem, count):
        @pl.when(count > 0)
        def _():
            pl.semaphore_wait(sem, count)

    def flag(value):
        return jnp.where(value, 1, 0)

    earlier_plane = (1 - core) + xi + rank(yi)
    later_plane = nx + ny - 1 - earlier_plane
    greetings = (
        place_in + earlier_plane + flag(high) * (nz - gs)
        + flag((group > 0) & (group < ng - 1)) * (1 + gs * flag(bottom))
    )
    if ng == 4:
        greetings = greetings + flag(group == 2) * (1 + gs * flag(top))

    up = jnp.where(iota((L, L), 0) <= iota((L, L), 1), 1.0, 0.0).astype(BF16)
    down = jnp.where(iota((L, L), 0) >= iota((L, L), 1), 1.0, 0.0).astype(BF16)
    parts = split3(lav[...])
    sums = nn(jnp.concatenate([*parts, jnp.zeros((8, L), F32)], axis=0).astype(BF16), up)
    cums = sums[0:8] + sums[8:16] + sums[16:24]
    tot = jnp.broadcast_to(cums[:, L - 1 : L], (8, L))
    after = jnp.exp(cums)
    before = jnp.exp(tot - cums)
    chunk_decay = jnp.exp(tot)
    tots = [tot[c : c + 1] for c in range(8)]
    run = jnp.zeros((1, L), F32)
    for c in range(8):
        scale_v[0, c] = jnp.broadcast_to(jnp.exp(run), (8, L))
        run = run + tots[c]
    device_decay = jnp.exp(run)
    run = jnp.zeros((1, L), F32)
    for c in reversed(range(8)):
        scale_v[1, c] = jnp.broadcast_to(jnp.exp(run), (8, L))
        run = run + tots[c]
    decay_tile = jnp.broadcast_to(device_decay, (8, L))

    def in_group(buf, sems, q):
        return pltpu.make_async_remote_copy(
            src_ref=buf.at[place_in], dst_ref=buf.at[place_in], send_sem=sems[0].at[q], recv_sem=sems[1].at[place_in],
            device_id=at_z(group * gs + q), device_id_type=MESH,
        )

    def arrived(buf, sems, q):
        pltpu.make_async_remote_copy(
            src_ref=buf.at[q], dst_ref=buf.at[q], send_sem=sems[0].at[q], recv_sem=sems[1].at[q],
            device_id=twin, device_id_type=MESH,
        ).wait_recv()

    g_sems, s_sems = (g_ss, g_rs), (s_ss, s_rs)

    def takes_g(q):
        return (q < place_in) | ((q == gs - 1) & wraps & (q != place_in))

    def takes_s(q):
        return (q > place_in) | ((q == 0) & (group == 0) & (q != place_in))

    loads[0].wait()
    loads[1].wait()
    back = jnp.zeros((64, L), F32)
    for c in reversed(range(8)):
        part = slice(c * L, (c + 1) * L)
        hi, lo = split2(dyv[:, part].astype(F32) * after[c : c + 1])
        cm = bcv[part, L : 2 * L]
        st_loc[1, c] = back
        back = back * chunk_decay[c : c + 1] + nn(
            jnp.concatenate([hi, lo], axis=1), jnp.concatenate([cm, cm], axis=0)
        )
    g_in[place_in, 0:64] = back
    g_in[place_in, 64:72] = decay_tile

    await_count(barrier, greetings)
    for q in range(gs):
        signal(ready_g, at_z(group * gs + q), q < place_in)
    signal(ready_w, at_z(below + gs - 1), group > 0)
    signal(ready_w, at_z(0), high)
    if ng == 4:
        signal(ready_w, at_z(lax.rem(group + 2, ng) * gs + gs - 1), group > 1)
    for device, later in pairs:
        signal(ready_p, device, jnp.logical_not(later))

    for q in range(gs):

        @pl.when(takes_g(q) & (q < place_in))
        def _():
            in_group(g_in, g_sems, q).start()

    loads[2].wait()
    state = jnp.zeros((64, L), F32)
    for c in range(8):
        part = slice(c * L, (c + 1) * L)
        hi, lo = split2(xv[:, part].astype(F32) * before[c : c + 1])
        bm = bcv[part, 0:L]
        st_loc[0, c] = state
        state = state * chunk_decay[c : c + 1] + nn(
            jnp.concatenate([hi, lo], axis=1), jnp.concatenate([bm, bm], axis=0)
        )
    st_loc[0, 8] = state
    s_in[place_in, 0:64] = state
    s_in[place_in, 64:72] = decay_tile

    @pl.when(takes_s(0))
    def _():
        in_group(s_in, s_sems, 0).start()

    await_count(ready_g, gs - 1 - place_in)

    @pl.when(takes_g(gs - 1))
    def _():
        in_group(g_in, g_sems, gs - 1).start()

    for q in range(1, gs):

        @pl.when(takes_s(q))
        def _():
            in_group(s_in, s_sems, q).start()

    def spans():
        return [(o, 2 * o <= ng) for o in range(1, ng)]

    def whole_copy(o, q):
        to = lax.rem(group + o, ng)
        kind = 1 - (group + o) // ng
        return pltpu.make_async_remote_copy(
            src_ref=whole_s.at[kind], dst_ref=whole_r.at[group], send_sem=w_ss.at[o, q], recv_sem=w_rs.at[group],
            device_id=at_z(to * gs + q), device_id_type=MESH,
        )

    def sender(up):
        return place_in == (gs - 1 if up else 0)

    collects_g = (bottom & (group > 0)) | (top & wraps)
    collects_s = low | (top & (group < ng - 1))

    @pl.when(collects_g)
    def _():
        for q in range(gs):

            @pl.when(q != place_in)
            def _():
                arrived(g_in, g_sems, q)

        decay = jnp.ones((8, L), F32)
        total = jnp.zeros((64, L), F32)
        for q in reversed(range(gs)):
            total = g_in[q, 0:64] + scaled(total, g_in[q, 64:72])
            decay = decay * g_in[q, 64:72]
        whole_s[0, 0:64] = total
        whole_s[0, 64:72] = decay
        for o, up in spans():
            for q in range(gs):

                @pl.when(sender(up) & (lax.rem(group + o, ng) < group))
                def _():
                    whole_copy(o, q).start()

    big = jnp.concatenate([cums, after, before, jnp.zeros((L - 24, L), F32)], axis=0).T
    lower = iota((L, L), 0) >= iota((L, L), 1)
    upper = iota((L, L), 0) <= iota((L, L), 1)
    rows_v[0] = after
    rows_v[1] = before

    def local(c):
        part = slice(c * L, (c + 1) * L)
        bm, cm = bcv[part, 0:L], bcv[part, L : 2 * L]
        xt, dyt = xv[:, part], dyv[:, part]
        xf, dyf = xt.astype(F32), dyt.astype(F32)
        x2 = jnp.concatenate([xf, xf], axis=0).T.astype(BF16)
        dy2 = jnp.concatenate([dyf, dyf], axis=0).T.astype(BF16)
        xyd[0, c] = dy2
        xyd[1, c] = x2
        col = jnp.broadcast_to(big[:, c : c + 1], (L, L))
        col_v[0, c] = jnp.broadcast_to(big[:, 8 + c : 9 + c], (L, L))
        col_v[1, c] = jnp.broadcast_to(big[:, 16 + c : 17 + c], (L, L))
        row = jnp.broadcast_to(cums[c : c + 1], (L, L))
        m = jnp.exp(jnp.where(lower, col - row, -1e30))
        mt = jnp.exp(jnp.where(upper, row - col, -1e30))
        w = split2(m * nt(cm, bm))
        q = split2(m * nn(dy2[:, 0:64], xt))
        qt = split2(mt * nn(x2[:, 0:64], dyt))
        loc_bc[1, c] = nn(jnp.concatenate(qt, axis=1), jnp.concatenate([cm, cm], axis=0))
        loc_bc[0, c] = nn(jnp.concatenate(q, axis=1), jnp.concatenate([bm, bm], axis=0))
        y_loc[c] = nt(jnp.concatenate([xt, xt], axis=1), jnp.concatenate(w, axis=1))
        dx_loc[c] = nn(jnp.concatenate([dyt, dyt], axis=1), jnp.concatenate(w, axis=0))

    for c in range(8):
        local(c)

    @pl.when(collects_s)
    def _():
        for q in range(gs):

            @pl.when(q != place_in)
            def _():
                arrived(s_in, s_sems, q)

        decay = jnp.ones((8, L), F32)
        total = jnp.zeros((64, L), F32)
        for q in range(gs):
            total = s_in[q, 0:64] + scaled(total, s_in[q, 64:72])
            decay = decay * s_in[q, 64:72]
        whole_s[1, 0:64] = total
        whole_s[1, 64:72] = decay
        told = gs * flag(top) + gs * flag(low)
        if ng == 4:
            told = told + gs * flag(top & (group < 2))
        await_count(ready_w, told)
        for o, up in spans():
            for q in range(gs):

                @pl.when(sender(up) & (lax.rem(group + o, ng) > group))
                def _():
                    whole_copy(o, q).start()

    ns_rows = nz * plan.slots
    owner_row = ownv[...]
    named = jnp.where(iota((16, NQ), 0) == owner_row, 1.0, 0.0)
    earlier = jnp.where(iota((NQ, NQ), 0) < iota((NQ, NQ), 1), 1.0, 0.0)
    rank = jnp.sum(named * nn(named.astype(BF16), earlier.astype(BF16)), axis=0, keepdims=True)
    slot = owner_row.astype(F32) * plan.slots + rank
    spread = jnp.where(iota((NQ, 1024), 0) == iota((NQ, 1024), 1) // NQ, 1.0, 0.0).astype(BF16)
    slot_t = nn(jnp.broadcast_to(slot, (16, NQ)).astype(BF16), spread)
    for c in range(8):
        hit = slot_t[0:1, c * L : (c + 1) * L] == iota((ns_rows, L), 0).astype(F32)
        place_v[c] = jnp.where(hit, 1.0, 0.0).astype(BF16)
    hit = slot == iota((ns_rows, NQ), 0).astype(F32)
    ids = jnp.sum(jnp.where(hit, locv[...].astype(F32) + 1.0, 0.0), axis=1, keepdims=True)
    ids_v[...] = jnp.where(iota((ns_rows, L), 1) >= 64, ids, 0.0)

    def whole_arrived(a):
        pltpu.make_async_remote_copy(
            src_ref=whole_s.at[0], dst_ref=whole_r.at[a], send_sem=w_ss.at[0, 0], recv_sem=w_rs.at[a],
            device_id=twin, device_id_type=MESH,
        ).wait_recv()

    def state_edge():
        edge_v[0] = jnp.zeros((64, L), F32)
        for a in range(ng):

            @pl.when(a < group)
            def _():
                whole_arrived(a)
                edge_v[0] = whole_r[a, 0:64] + scaled(edge_v[0], whole_r[a, 64:72])

        for q in range(gs):

            @pl.when((q < place_in) & jnp.logical_not(collects_s))
            def _():
                arrived(s_in, s_sems, q)

            @pl.when(q < place_in)
            def _():
                edge_v[0] = s_in[q, 0:64] + scaled(edge_v[0], s_in[q, 64:72])

    def gradient_edge():
        edge_v[1] = jnp.zeros((64, L), F32)
        for a in reversed(range(ng)):

            @pl.when(a > group)
            def _():
                whole_arrived(a)
                edge_v[1] = whole_r[a, 0:64] + scaled(edge_v[1], whole_r[a, 64:72])

        for q in reversed(range(gs)):

            @pl.when((q > place_in) & jnp.logical_not(collects_g))
            def _():
                arrived(g_in, g_sems, q)

            @pl.when(q > place_in)
            def _():
                edge_v[1] = g_in[q, 0:64] + scaled(edge_v[1], g_in[q, 64:72])

    def with_edge(kind, c, edge):
        return st_loc[kind, c] + scaled(edge, scale_v[kind, c])

    span = plan.chunks
    steps = [lax.rem(xi + d, nx) for d in ([2, 1, 3] if nx == 4 else range(1, nx))] + [xi]
    order = [t * span + i for t in steps for i in range(span)]

    def core_copy(kind, c, k):
        return pltpu.make_async_remote_copy(
            src_ref=dbc.at[kind, c, :, 1 - core], dst_ref=crecv.at[kind, c],
            send_sem=c_ss.at[kind, k], recv_sem=c_rs.at[kind, k], device_id=twin, device_id_type=MESH,
        )

    def x_copy(kind, to):
        return pltpu.make_async_remote_copy(
            src_ref=csum.at[kind, pl.ds(to * span, span)], dst_ref=xrecv.at[kind, xi],
            send_sem=x_ss.at[kind, to], recv_sem=x_rs.at[kind, xi],
            device_id=at_head(head(to, yi, core)), device_id_type=MESH,
        )

    def y_copy(kind, d):
        to = lax.rem(yi + d, ny)
        return pltpu.make_async_remote_copy(
            src_ref=ysum.at[kind, to], dst_ref=yrecv.at[kind, yi], send_sem=y_ss.at[kind, d], recv_sem=y_rs.at[kind, yi],
            device_id=at_head(head(xi, to, core)), device_id_type=MESH,
        )

    def over_cores_and_out(kind):
        for n, to in enumerate(steps):
            for i in range(span):
                k = n * span + i
                c = order[k]
                core_copy(kind, c, k).wait_recv()
                csum[kind, c] = dbc[kind, c, :, core] + crecv[kind, c]
            if n < nx - 1:
                x_copy(kind, to).start()

    news_order = sorted(range(1, nz), key=lambda d: -min(d, nz - d))
    y_order = sorted(range(1, ny), key=lambda d: -min(d, ny - d))

    def over_x_and_out(kind):
        total = csum[kind, pl.ds(xi * span, span)]
        for d in range(1, nx):
            source = lax.rem(xi + d, nx)
            pltpu.make_async_remote_copy(
                src_ref=xrecv.at[kind, source], dst_ref=xrecv.at[kind, source],
                send_sem=x_ss.at[kind, 0], recv_sem=x_rs.at[kind, source], device_id=twin, device_id_type=MESH,
            ).wait_recv()
            total = total + xrecv[kind, source]
        ysum[kind] = total.reshape(ny, plan.block, L)
        for d in y_order:
            y_copy(kind, d).start()

    def over_y(kind):
        total = ysum[kind, yi]
        for d in y_order:
            source = lax.rem(yi + d, ny)
            pltpu.make_async_remote_copy(
                src_ref=ysum.at[kind, 0], dst_ref=yrecv.at[kind, source],
                send_sem=y_ss.at[kind, 0], recv_sem=y_rs.at[kind, source], device_id=twin, device_id_type=MESH,
            ).wait_recv()
            total = total + yrecv[kind, source]
        bcg_ref[:, pl.ds(pl.multiple_of((1 - kind) * L, L), L)] = total

    def finish_dx(c, acc):
        part = slice(c * L, (c + 1) * L)
        dxs = nt(st2[1, c], bcv[part, 0:L])
        dxt = dx_loc[c] + rows_v[1, c : c + 1] * (dxs[0:64] + dxs[64:128])
        hi, lo = split2(dxt)
        xg_ref[:, part] = hi
        none = jnp.zeros((64, L), BF16)
        both = jnp.concatenate(
            [jnp.concatenate([hi, none], axis=0), jnp.concatenate([lo, none], axis=0)], axis=1
        )
        place = place_v[c]
        vx_v[c : c + 1] = jnp.sum(xv[:, part].astype(F32) * dxt, axis=0, keepdims=True)
        return acc + nt(jnp.concatenate([place, place], axis=1), both)

    def news_copy(d):
        to = lax.rem(zi + d, nz)
        return pltpu.make_async_remote_copy(
            src_ref=ns.at[to], dst_ref=nr.at[zi], send_sem=n_ss.at[d], recv_sem=n_rs.at[zi],
            device_id=at_z(to), device_id_type=MESH,
        )

    await_count(ready_p, later_plane)
    first = (group + 1) // ng
    shape = (plan.blocks, 2, plan.block, L)

    def phase(i, carried):
        kind = first + i - 2 * first * i
        pl.when(kind == 0)(state_edge)
        pl.when(kind == 1)(gradient_edge)
        edge = edge_v[kind]
        for k, c in enumerate(order):
            st = jnp.concatenate(split2(with_edge(kind, c, edge)), axis=0)
            st2[kind, c] = st
            dbc[kind, c] = (loc_bc[kind, c] + col_v[kind, c] * nn(xyd[kind, c], st)).reshape(shape)
            core_copy(kind, c, k).start()
        @pl.when(kind == 1)
        def _():
            acc = ids_v[...]
            for c in range(8):
                acc = finish_dx(c, acc)
            ns[...] = acc.reshape(nz, plan.slots, L)
            for d in news_order:
                news_copy(d).start()
            nr[zi] = ns[zi]

        over_cores_and_out(kind)
        over_x_and_out(kind)
        return carried

    lax.fori_loop(0, 2, phase, 0)

    start, carry = edge_v[0], edge_v[1]
    for c in range(8):
        part = slice(c * L, (c + 1) * L)
        ys = nt(st2[0, c], bcv[part, L : 2 * L])
        yt = y_loc[c] + rows_v[0, c : c + 1] * (ys[0:64] + ys[64:128])
        vy = jnp.sum(dyv[:, part].astype(F32) * yt, axis=0, keepdims=True)
        if c < 7:
            end = with_edge(0, c + 1, start)
        else:
            end = st_loc[0, 8] + scaled(start, decay_tile)
        ve[c : c + 1, 0:L] = vy - vx_v[c : c + 1]
        ve[c : c + 1, L : 2 * L] = jnp.sum(with_edge(1, c, carry) * end, axis=0, keepdims=True)
    parts = split3(ve[...])
    sums = nn(
        jnp.concatenate([*parts, jnp.zeros((8, 2 * L), F32)], axis=0).astype(BF16),
        jnp.concatenate([down, jnp.ones((L, L), BF16)], axis=0),
    )
    dla_ref[...] = sums[0:8] + sums[8:16] + sums[16:24]
    over_y(first)

    for d in range(1, nz):
        source = lax.rem(zi + nz - d, nz)
        pltpu.make_async_remote_copy(
            src_ref=ns.at[0], dst_ref=nr.at[source], send_sem=n_ss.at[d], recv_sem=n_rs.at[source],
            device_id=at_z(source), device_id_type=MESH,
        ).wait_recv()
    tiles = nr[...].reshape(ns_rows, L)
    lane = iota((ns_rows, L), 1)
    row_hit = jnp.where((lane >= 64) & (tiles == (lane - 63).astype(F32)), 1.0, 0.0).T.astype(BF16)
    hi, lo = split2(tiles)
    news_ref[...] = (nn(row_hit, hi) + nn(row_hit, lo))[64:128, 0:64]

    over_y(1 - first)

    for q in range(gs):

        @pl.when(takes_g(q))
        def _():
            in_group(g_in, g_sems, q).wait_send()

        @pl.when(takes_s(q))
        def _():
            in_group(s_in, s_sems, q).wait_send()

        for o, up in spans():

            @pl.when(sender(up))
            def _():
                whole_copy(o, q).wait_send()

    for d in range(1, nz):
        news_copy(d).wait_send()
    for kind in range(2):
        for k, c in enumerate(order):
            core_copy(kind, c, k).wait_send()
        for to in steps[:-1]:
            x_copy(kind, to).wait_send()
        for d in range(1, ny):
            y_copy(kind, d).wait_send()


def write_out(a, b, c, d, a_out, b_out, c_out, d_out, sems):
    pairs = ((a, a_out), (b, b_out), (c, c_out), (d, d_out))
    copies = [pltpu.make_async_copy(src, dst, sems.at[k]) for k, (src, dst) in enumerate(pairs)]
    for copy in copies:
        copy.start()
    for copy in copies:
        copy.wait()


def on_device(plan, xs, bc, log_decay, out_grad, news_owner, news_local):
    rows = plan.tm * plan.slots
    dma = pltpu.SemaphoreType.DMA
    vm = pltpu.VMEM
    shapes = (
        jax.ShapeDtypeStruct((64, 1024), BF16),
        jax.ShapeDtypeStruct((plan.block, 2 * L), F32),
        jax.ShapeDtypeStruct((8, L), F32),
        jax.ShapeDtypeStruct((NEWS_DEV, 64), F32),
    )
    slab = (plan.blocks, plan.block, L)
    ng, gs, nx, ny = plan.groups, plan.size, plan.x, plan.y
    scratch = [
        vm((64, 1024), BF16), vm((64, 1024), BF16), vm((1024, 2 * L), BF16),
        vm((2, 8, L, L), BF16), vm((2, 8, L, L), F32), vm((2, 9, 64, L), F32), vm((2, 8, 8, L), F32), vm((2, 8, L), F32),
        vm((2, 8, L, L), F32), vm((2, 8, plan.blocks, 2, plan.block, L), F32),
        vm((2, 8, *slab), F32), vm((2, 8, *slab), F32), vm((2, nx, plan.chunks, *slab), F32),
        vm((2, ny, plan.block, L), F32), vm((2, ny, plan.block, L), F32),
        vm((8, 64, L), F32), vm((8, 64, L), F32), vm((2, 8, L, L), BF16),
        vm((8, rows, L), BF16), vm((rows, L), F32), vm((8, L), F32), vm((8, 2 * L), F32),
        vm((gs, 72, L), F32), vm((gs, 72, L), F32), vm((2, 72, L), F32), vm((ng, 72, L), F32), vm((2, 64, L), F32),
        vm((plan.tm, plan.slots, L), F32), vm((plan.tm, plan.slots, L), F32),
        *[pltpu.SemaphoreType.REGULAR] * 3, dma((3,)),
        dma((gs,)), dma((gs,)), dma((gs,)), dma((gs,)), dma((ng, gs)), dma((ng,)),
        dma((2, 8)), dma((2, 8)), dma((2, nx)), dma((2, nx)), dma((2, ny)), dma((2, ny)),
        dma((plan.tm,)), dma((plan.tm,)),
    ]
    anywhere = pl.BlockSpec(memory_space=pl.ANY)
    vmem = pl.BlockSpec(memory_space=pltpu.VMEM)
    results = pl.pallas_call(
        functools.partial(kernel, plan),
        out_shape=shapes,
        in_specs=[anywhere] * 3 + [vmem] * 3,
        out_specs=(vmem,) * 4,
        scratch_shapes=scratch,
        compiler_params=pltpu.CompilerParams(
            collective_id=0, has_side_effects=True, vmem_limit_bytes=55000 * 1024
        ),
    )(
        xs.T, out_grad.T, bc, log_decay.reshape(8, L), news_owner.reshape(1, NQ), news_local.reshape(1, NQ)
    )
    xg, bcg, dla, news = pl.pallas_call(
        write_out,
        out_shape=shapes,
        in_specs=[anywhere] * 4,
        out_specs=(anywhere,) * 4,
        scratch_shapes=[dma((4,))],
        compiler_params=pltpu.CompilerParams(vmem_limit_bytes=2**20),
    )(*results)
    return xg.T, bcg, dla.reshape(1024, 1), news


def solution(mesh):
    tm, heads = mesh.shape["tm"], mesh.shape["head"]
    plan = Plan(tm, 3, 4, heads // 8, 8 if tm == 12 else 32)
    return jax.shard_map(
        functools.partial(on_device, plan),
        mesh=mesh,
        in_specs=(
            P("tm", "head"), P("tm", None), P("tm", "head"), P("tm", "head"), P("tm", None), P("tm", None),
        ),
        out_specs=(P("tm", "head"), P(("tm", "head"), None), P("tm", "head"), P("tm", "head")),
        check_vma=False,
    )
```

```python
import functools

import jax
import jax.numpy as jnp
from jax import lax
from jax.experimental import pallas as pl
from jax.experimental.pallas import tpu as pltpu
from jax.sharding import PartitionSpec as P

MESH = pl.DeviceIdType.MESH
F32 = jnp.float32
BF16 = jnp.bfloat16
NEWS_DEV = 64
NQ = 32
L = 128


def nn(a, b):
    return lax.dot_general(a, b, (((1,), (0,)), ((), ())), preferred_element_type=F32)


def nt(a, b):
    return lax.dot_general(a, b, (((1,), (1,)), ((), ())), preferred_element_type=F32)


def split2(v):
    hi = v.astype(BF16)
    return hi, (v - hi.astype(F32)).astype(BF16)


def split3(v):
    one = v.astype(BF16).astype(F32)
    two = (v - one).astype(BF16).astype(F32)
    return one, two, v - one - two


def scaled(tiles, tile):
    return (tiles.reshape(8, 8, L) * tile[None]).reshape(64, L)


def iota(shape, dim):
    return lax.broadcasted_iota(jnp.int32, shape, dim)


class Plan:
    def __init__(self, tm, groups, x, y, slots):
        self.tm, self.groups, self.x, self.y, self.slots = tm, groups, x, y, slots
        self.size = tm // groups
        self.block = 1024 // (x * y * 2)
        self.blocks = L // (2 * self.block)
        self.chunks = 8 // x


def kernel(
    plan,
    x_hbm, dy_hbm, bc_hbm, lav, ownv, locv,
    xg_ref, bcg_ref, dla_ref, news_ref,
    xv, dyv, bcv,
    xyd, col_v, st_loc, scale_v, rows_v,
    loc_bc, dbc, crecv, csum, xrecv, ysum, yrecv,
    y_loc, dx_loc, st2, place_v, ids_v, vx_v, ve,
    g_in, s_in, whole_s, whole_r, edge_v, ns, nr,
    ready_g, ready_w, ready_p, in_sem, g_ss, g_rs, s_ss, s_rs, w_ss, w_rs,
    c_ss, c_rs, x_ss, x_rs, y_ss, y_rs, n_ss, n_rs,
):
    nz, ny, nx = plan.tm, plan.y, plan.x
    zi = lax.axis_index("tm")
    hi_ = lax.axis_index("head")
    core = lax.rem(hi_, 2)
    yi = lax.rem(hi_ // 2, ny)
    xi = hi_ // (2 * ny)

    def head(x, y, c):
        return (x * ny + y) * 2 + c

    def at_z(z):
        return (z, hi_)

    def at_head(h):
        return (zi, h)

    ng, gs = plan.groups, plan.size
    group, place_in = zi // gs, lax.rem(zi, gs)
    twin = at_head(head(xi, yi, 1 - core))

    loads = [
        pltpu.make_async_copy(src, dst, in_sem.at[k])
        for k, (src, dst) in enumerate(
            ((dy_hbm, dyv), (bc_hbm, bcv), (x_hbm, xv))
        )
    ]
    for load in loads:
        load.start()

    barrier = pltpu.get_barrier_semaphore()
    low, high = zi == 0, group == ng - 1
    wraps = group >= ng - ng // 2
    bottom, top = place_in == 0, place_in == gs - 1

    def rank(y):
        return y + y // (ny // 2) * (ny + ny // 2 - 1 - 2 * y)

    def signal(sem, device, when):
        @pl.when(when)
        def _():
            pl.semaphore_signal(sem, inc=1, device_id=device, device_id_type=MESH)

    pairs = [(twin, core == 1)]
    for d in range(1, nx):
        to = lax.rem(xi + d, nx)
        pairs.append((at_head(head(to, yi, core)), to > xi))
    for d in range(1, ny):
        to = lax.rem(yi + d, ny)
        pairs.append((at_head(head(xi, to, core)), rank(to) > rank(yi)))

    for q in range(gs):
        signal(barrier, at_z(group * gs + q), q > place_in)
    above = lax.rem(group + 1, ng) * gs
    below = lax.rem(group + ng - 1, ng) * gs
    signal(barrier, at_z(above), group + 1 < ng - 1)
    for q in range(gs):
        signal(barrier, at_z(above + q), top & (group + 1 < ng - 1))
        signal(barrier, at_z(nz - gs + q), group < ng - 1)
    if ng == 4:
        signal(barrier, at_z(3 * gs - 1), group == 0)
        for q in range(gs):
            signal(barrier, at_z(2 * gs + q), top & (group == 0))
    for device, later in pairs:
        signal(barrier, device, later)

    def await_count(sem, count):
        @pl.when(count > 0)
        def _():
            pl.semaphore_wait(sem, count)

    def flag(value):
        return jnp.where(value, 1, 0)

    earlier_plane = (1 - core) + xi + rank(yi)
    later_plane = nx + ny - 1 - earlier_plane
    greetings = (
        place_in + earlier_plane + flag(high) * (nz - gs)
        + flag((group > 0) & (group < ng - 1)) * (1 + gs * flag(bottom))
    )
    if ng == 4:
        greetings = greetings + flag(group == 2) * (1 + gs * flag(top))

    up = jnp.where(iota((L, L), 0) <= iota((L, L), 1), 1.0, 0.0).astype(BF16)
    down = jnp.where(iota((L, L), 0) >= iota((L, L), 1), 1.0, 0.0).astype(BF16)
    parts = split3(lav[...])
    sums = nn(jnp.concatenate([*parts, jnp.zeros((8, L), F32)], axis=0).astype(BF16), up)
    cums = sums[0:8] + sums[8:16] + sums[16:24]
    tot = jnp.broadcast_to(cums[:, L - 1 : L], (8, L))
    after = jnp.exp(cums)
    before = jnp.exp(tot - cums)
    chunk_decay = jnp.exp(tot)
    tots = [tot[c : c + 1] for c in range(8)]
    run = jnp.zeros((1, L), F32)
    for c in range(8):
        scale_v[0, c] = jnp.broadcast_to(jnp.exp(run), (8, L))
        run = run + tots[c]
    device_decay = jnp.exp(run)
    run = jnp.zeros((1, L), F32)
    for c in reversed(range(8)):
        scale_v[1, c] = jnp.broadcast_to(jnp.exp(run), (8, L))
        run = run + tots[c]
    decay_tile = jnp.broadcast_to(device_decay, (8, L))

    def in_group(buf, sems, q):
        return pltpu.make_async_remote_copy(
            src_ref=buf.at[place_in], dst_ref=buf.at[place_in], send_sem=sems[0].at[q], recv_sem=sems[1].at[place_in],
            device_id=at_z(group * gs + q), device_id_type=MESH,
        )

    def arrived(buf, sems, q):
        pltpu.make_async_remote_copy(
            src_ref=buf.at[q], dst_ref=buf.at[q], send_sem=sems[0].at[q], recv_sem=sems[1].at[q],
            device_id=twin, device_id_type=MESH,
        ).wait_recv()

    g_sems, s_sems = (g_ss, g_rs), (s_ss, s_rs)

    def takes_g(q):
        return (q < place_in) | ((q == gs - 1) & wraps & (q != place_in))

    def takes_s(q):
        return (q > place_in) | ((q == 0) & (group == 0) & (q != place_in))

    loads[0].wait()
    loads[1].wait()
    back = jnp.zeros((64, L), F32)
    for c in reversed(range(8)):
        part = slice(c * L, (c + 1) * L)
        hi, lo = split2(dyv[:, part].astype(F32) * after[c : c + 1])
        cm = bcv[part, L : 2 * L]
        st_loc[1, c] = back
        back = back * chunk_decay[c : c + 1] + nn(
            jnp.concatenate([hi, lo], axis=1), jnp.concatenate([cm, cm], axis=0)
        )
    g_in[place_in, 0:64] = back
    g_in[place_in, 64:72] = decay_tile

    await_count(barrier, greetings)
    for q in range(gs):
        signal(ready_g, at_z(group * gs + q), q < place_in)
    signal(ready_w, at_z(below + gs - 1), group > 0)
    signal(ready_w, at_z(0), high)
    if ng == 4:
        signal(ready_w, at_z(lax.rem(group + 2, ng) * gs + gs - 1), group > 1)
    for device, later in pairs:
        signal(ready_p, device, jnp.logical_not(later))

    for q in range(gs):

        @pl.when(takes_g(q) & (q < place_in))
        def _():
            in_group(g_in, g_sems, q).start()

    loads[2].wait()
    state = jnp.zeros((64, L), F32)
    for c in range(8):
        part = slice(c * L, (c + 1) * L)
        hi, lo = split2(xv[:, part].astype(F32) * before[c : c + 1])
        bm = bcv[part, 0:L]
        st_loc[0, c] = state
        state = state * chunk_decay[c : c + 1] + nn(
            jnp.concatenate([hi, lo], axis=1), jnp.concatenate([bm, bm], axis=0)
        )
    st_loc[0, 8] = state
    s_in[place_in, 0:64] = state
    s_in[place_in, 64:72] = decay_tile

    @pl.when(takes_s(0))
    def _():
        in_group(s_in, s_sems, 0).start()

    await_count(ready_g, gs - 1 - place_in)

    @pl.when(takes_g(gs - 1))
    def _():
        in_group(g_in, g_sems, gs - 1).start()

    for q in range(1, gs):

        @pl.when(takes_s(q))
        def _():
            in_group(s_in, s_sems, q).start()

    def spans():
        return [(o, 2 * o <= ng) for o in range(1, ng)]

    def whole_copy(o, q):
        to = lax.rem(group + o, ng)
        kind = 1 - (group + o) // ng
        return pltpu.make_async_remote_copy(
            src_ref=whole_s.at[kind], dst_ref=whole_r.at[group], send_sem=w_ss.at[o, q], recv_sem=w_rs.at[group],
            device_id=at_z(to * gs + q), device_id_type=MESH,
        )

    def sender(up):
        return place_in == (gs - 1 if up else 0)

    collects_g = (bottom & (group > 0)) | (top & wraps)
    collects_s = low | (top & (group < ng - 1))

    @pl.when(collects_g)
    def _():
        for q in range(gs):

            @pl.when(q != place_in)
            def _():
                arrived(g_in, g_sems, q)

        decay = jnp.ones((8, L), F32)
        total = jnp.zeros((64, L), F32)
        for q in reversed(range(gs)):
            total = g_in[q, 0:64] + scaled(total, g_in[q, 64:72])
            decay = decay * g_in[q, 64:72]
        whole_s[0, 0:64] = total
        whole_s[0, 64:72] = decay
        for o, up in spans():
            for q in range(gs):

                @pl.when(sender(up) & (lax.rem(group + o, ng) < group))
                def _():
                    whole_copy(o, q).start()

    big = jnp.concatenate([cums, after, before, jnp.zeros((L - 24, L), F32)], axis=0).T
    lower = iota((L, L), 0) >= iota((L, L), 1)
    upper = iota((L, L), 0) <= iota((L, L), 1)
    rows_v[0] = after
    rows_v[1] = before

    def local(c):
        part = slice(c * L, (c + 1) * L)
        bm, cm = bcv[part, 0:L], bcv[part, L : 2 * L]
        xt, dyt = xv[:, part], dyv[:, part]
        xf, dyf = xt.astype(F32), dyt.astype(F32)
        x2 = jnp.concatenate([xf, xf], axis=0).T.astype(BF16)
        dy2 = jnp.concatenate([dyf, dyf], axis=0).T.astype(BF16)
        xyd[0, c] = dy2
        xyd[1, c] = x2
        col = jnp.broadcast_to(big[:, c : c + 1], (L, L))
        col_v[0, c] = jnp.broadcast_to(big[:, 8 + c : 9 + c], (L, L))
        col_v[1, c] = jnp.broadcast_to(big[:, 16 + c : 17 + c], (L, L))
        row = jnp.broadcast_to(cums[c : c + 1], (L, L))
        m = jnp.exp(jnp.where(lower, col - row, -1e30))
        mt = jnp.exp(jnp.where(upper, row - col, -1e30))
        w = split2(m * nt(cm, bm))
        q = split2(m * nn(dy2[:, 0:64], xt))
        qt = split2(mt * nn(x2[:, 0:64], dyt))
        loc_bc[1, c] = nn(jnp.concatenate(qt, axis=1), jnp.concatenate([cm, cm], axis=0))
        loc_bc[0, c] = nn(jnp.concatenate(q, axis=1), jnp.concatenate([bm, bm], axis=0))
        y_loc[c] = nt(jnp.concatenate([xt, xt], axis=1), jnp.concatenate(w, axis=1))
        dx_loc[c] = nn(jnp.concatenate([dyt, dyt], axis=1), jnp.concatenate(w, axis=0))

    for c in range(8):
        local(c)

    @pl.when(collects_s)
    def _():
        for q in range(gs):

            @pl.when(q != place_in)
            def _():
                arrived(s_in, s_sems, q)

        decay = jnp.ones((8, L), F32)
        total = jnp.zeros((64, L), F32)
        for q in range(gs):
            total = s_in[q, 0:64] + scaled(total, s_in[q, 64:72])
            decay = decay * s_in[q, 64:72]
        whole_s[1, 0:64] = total
        whole_s[1, 64:72] = decay
        told = gs * flag(top) + gs * flag(low)
        if ng == 4:
            told = told + gs * flag(top & (group < 2))
        await_count(ready_w, told)
        for o, up in spans():
            for q in range(gs):

                @pl.when(sender(up) & (lax.rem(group + o, ng) > group))
                def _():
                    whole_copy(o, q).start()

    ns_rows = nz * plan.slots
    owner_row = ownv[...]
    named = jnp.where(iota((16, NQ), 0) == owner_row, 1.0, 0.0)
    earlier = jnp.where(iota((NQ, NQ), 0) < iota((NQ, NQ), 1), 1.0, 0.0)
    rank = jnp.sum(named * nn(named.astype(BF16), earlier.astype(BF16)), axis=0, keepdims=True)
    slot = owner_row.astype(F32) * plan.slots + rank
    spread = jnp.where(iota((NQ, 1024), 0) == iota((NQ, 1024), 1) // NQ, 1.0, 0.0).astype(BF16)
    slot_t = nn(jnp.broadcast_to(slot, (16, NQ)).astype(BF16), spread)
    for c in range(8):
        hit = slot_t[0:1, c * L : (c + 1) * L] == iota((ns_rows, L), 0).astype(F32)
        place_v[c] = jnp.where(hit, 1.0, 0.0).astype(BF16)
    hit = slot == iota((ns_rows, NQ), 0).astype(F32)
    ids = jnp.sum(jnp.where(hit, locv[...].astype(F32) + 1.0, 0.0), axis=1, keepdims=True)
    ids_v[...] = jnp.where(iota((ns_rows, L), 1) >= 64, ids, 0.0)

    def whole_arrived(a):
        pltpu.make_async_remote_copy(
            src_ref=whole_s.at[0], dst_ref=whole_r.at[a], send_sem=w_ss.at[0, 0], recv_sem=w_rs.at[a],
            device_id=twin, device_id_type=MESH,
        ).wait_recv()

    def state_edge():
        edge_v[0] = jnp.zeros((64, L), F32)
        for a in range(ng):

            @pl.when(a < group)
            def _():
                whole_arrived(a)
                edge_v[0] = whole_r[a, 0:64] + scaled(edge_v[0], whole_r[a, 64:72])

        for q in range(gs):

            @pl.when((q < place_in) & jnp.logical_not(collects_s))
            def _():
                arrived(s_in, s_sems, q)

            @pl.when(q < place_in)
            def _():
                edge_v[0] = s_in[q, 0:64] + scaled(edge_v[0], s_in[q, 64:72])

    def gradient_edge():
        edge_v[1] = jnp.zeros((64, L), F32)
        for a in reversed(range(ng)):

            @pl.when(a > group)
            def _():
                whole_arrived(a)
                edge_v[1] = whole_r[a, 0:64] + scaled(edge_v[1], whole_r[a, 64:72])

        for q in reversed(range(gs)):

            @pl.when((q > place_in) & jnp.logical_not(collects_g))
            def _():
                arrived(g_in, g_sems, q)

            @pl.when(q > place_in)
            def _():
                edge_v[1] = g_in[q, 0:64] + scaled(edge_v[1], g_in[q, 64:72])

    def with_edge(kind, c, edge):
        return st_loc[kind, c] + scaled(edge, scale_v[kind, c])

    span = plan.chunks
    steps = [lax.rem(xi + d, nx) for d in ([2, 1, 3] if nx == 4 else range(1, nx))] + [xi]
    order = [t * span + i for i in range(span) for t in steps]

    def core_copy(kind, c, k):
        return pltpu.make_async_remote_copy(
            src_ref=dbc.at[kind, c, :, 1 - core], dst_ref=crecv.at[kind, c],
            send_sem=c_ss.at[kind, k], recv_sem=c_rs.at[kind, k], device_id=twin, device_id_type=MESH,
        )

    def x_copy(kind, to, i):
        return pltpu.make_async_remote_copy(
            src_ref=csum.at[kind, to * span + i], dst_ref=xrecv.at[kind, xi, i],
            send_sem=x_ss.at[kind, to * span + i], recv_sem=x_rs.at[kind, xi * span + i],
            device_id=at_head(head(to, yi, core)), device_id_type=MESH,
        )

    def y_copy(kind, d):
        to = lax.rem(yi + d, ny)
        return pltpu.make_async_remote_copy(
            src_ref=ysum.at[kind, to], dst_ref=yrecv.at[kind, yi], send_sem=y_ss.at[kind, d], recv_sem=y_rs.at[kind, yi],
            device_id=at_head(head(xi, to, core)), device_id_type=MESH,
        )

    def over_cores_and_out(kind):
        for k, c in enumerate(order):
            core_copy(kind, c, k).wait_recv()
            csum[kind, c] = dbc[kind, c, :, core] + crecv[kind, c]
            if k % nx < nx - 1:
                x_copy(kind, steps[k % nx], k // nx).start()

    news_order = sorted(range(1, nz), key=lambda d: -min(d, nz - d))
    y_order = sorted(range(1, ny), key=lambda d: -min(d, ny - d))

    def over_x_and_out(kind):
        for i in range(span):
            total = csum[kind, xi * span + i]
            for d in range(1, nx):
                source = lax.rem(xi + d, nx)
                pltpu.make_async_remote_copy(
                    src_ref=xrecv.at[kind, source, i], dst_ref=xrecv.at[kind, source, i], send_sem=x_ss.at[kind, 0],
                    recv_sem=x_rs.at[kind, source * span + i], device_id=twin, device_id_type=MESH,
                ).wait_recv()
                total = total + xrecv[kind, source, i]
            ysum[kind, i * plan.blocks : (i + 1) * plan.blocks] = total
            for d in y_order:

                @pl.when(lax.rem(yi + d, ny) // plan.blocks == i)
                def _():
                    y_copy(kind, d).start()

    def over_y(kind):
        total = ysum[kind, yi]
        for d in y_order:
            source = lax.rem(yi + d, ny)
            pltpu.make_async_remote_copy(
                src_ref=ysum.at[kind, 0], dst_ref=yrecv.at[kind, source],
                send_sem=y_ss.at[kind, 0], recv_sem=y_rs.at[kind, source], device_id=twin, device_id_type=MESH,
            ).wait_recv()
            total = total + yrecv[kind, source]
        bcg_ref[:, pl.ds(pl.multiple_of((1 - kind) * L, L), L)] = total

    def finish_dx(c, acc):
        part = slice(c * L, (c + 1) * L)
        dxs = nt(st2[1, c], bcv[part, 0:L])
        dxt = dx_loc[c] + rows_v[1, c : c + 1] * (dxs[0:64] + dxs[64:128])
        hi, lo = split2(dxt)
        xg_ref[:, part] = hi
        none = jnp.zeros((64, L), BF16)
        both = jnp.concatenate(
            [jnp.concatenate([hi, none], axis=0), jnp.concatenate([lo, none], axis=0)], axis=1
        )
        place = place_v[c]
        vx_v[c : c + 1] = jnp.sum(xv[:, part].astype(F32) * dxt, axis=0, keepdims=True)
        return acc + nt(jnp.concatenate([place, place], axis=1), both)

    def news_copy(d):
        to = lax.rem(zi + d, nz)
        return pltpu.make_async_remote_copy(
            src_ref=ns.at[to], dst_ref=nr.at[zi], send_sem=n_ss.at[d], recv_sem=n_rs.at[zi],
            device_id=at_z(to), device_id_type=MESH,
        )

    await_count(ready_p, later_plane)
    first = (group + 1) // ng
    shape = (plan.blocks, 2, plan.block, L)

    def phase(i, carried):
        kind = first + i - 2 * first * i
        pl.when(kind == 0)(state_edge)
        pl.when(kind == 1)(gradient_edge)
        edge = edge_v[kind]
        for k, c in enumerate(order):
            st = jnp.concatenate(split2(with_edge(kind, c, edge)), axis=0)
            st2[kind, c] = st
            dbc[kind, c] = (loc_bc[kind, c] + col_v[kind, c] * nn(xyd[kind, c], st)).reshape(shape)
            core_copy(kind, c, k).start()
        @pl.when(kind == 1)
        def _():
            acc = ids_v[...]
            for c in range(8):
                acc = finish_dx(c, acc)
            ns[...] = acc.reshape(nz, plan.slots, L)
            for d in news_order:
                news_copy(d).start()
            nr[zi] = ns[zi]

        over_cores_and_out(kind)
        over_x_and_out(kind)
        return carried

    lax.fori_loop(0, 2, phase, 0)

    start, carry = edge_v[0], edge_v[1]
    for c in range(8):
        part = slice(c * L, (c + 1) * L)
        ys = nt(st2[0, c], bcv[part, L : 2 * L])
        yt = y_loc[c] + rows_v[0, c : c + 1] * (ys[0:64] + ys[64:128])
        vy = jnp.sum(dyv[:, part].astype(F32) * yt, axis=0, keepdims=True)
        if c < 7:
            end = with_edge(0, c + 1, start)
        else:
            end = st_loc[0, 8] + scaled(start, decay_tile)
        ve[c : c + 1, 0:L] = vy - vx_v[c : c + 1]
        ve[c : c + 1, L : 2 * L] = jnp.sum(with_edge(1, c, carry) * end, axis=0, keepdims=True)
    parts = split3(ve[...])
    sums = nn(
        jnp.concatenate([*parts, jnp.zeros((8, 2 * L), F32)], axis=0).astype(BF16),
        jnp.concatenate([down, jnp.ones((L, L), BF16)], axis=0),
    )
    dla_ref[...] = sums[0:8] + sums[8:16] + sums[16:24]
    over_y(first)

    for d in range(1, nz):
        source = lax.rem(zi + nz - d, nz)
        pltpu.make_async_remote_copy(
            src_ref=ns.at[0], dst_ref=nr.at[source], send_sem=n_ss.at[d], recv_sem=n_rs.at[source],
            device_id=at_z(source), device_id_type=MESH,
        ).wait_recv()
    tiles = nr[...].reshape(ns_rows, L)
    lane = iota((ns_rows, L), 1)
    row_hit = jnp.where((lane >= 64) & (tiles == (lane - 63).astype(F32)), 1.0, 0.0).T.astype(BF16)
    hi, lo = split2(tiles)
    news_ref[...] = (nn(row_hit, hi) + nn(row_hit, lo))[64:128, 0:64]

    over_y(1 - first)

    for q in range(gs):

        @pl.when(takes_g(q))
        def _():
            in_group(g_in, g_sems, q).wait_send()

        @pl.when(takes_s(q))
        def _():
            in_group(s_in, s_sems, q).wait_send()

        for o, up in spans():

            @pl.when(sender(up))
            def _():
                whole_copy(o, q).wait_send()

    for d in range(1, nz):
        news_copy(d).wait_send()
    for kind in range(2):
        for k, c in enumerate(order):
            core_copy(kind, c, k).wait_send()
        for to in steps[:-1]:
            for i in range(span):
                x_copy(kind, to, i).wait_send()
        for d in range(1, ny):
            y_copy(kind, d).wait_send()


def write_out(a, b, c, d, a_out, b_out, c_out, d_out, sems):
    pairs = ((a, a_out), (b, b_out), (c, c_out), (d, d_out))
    copies = [pltpu.make_async_copy(src, dst, sems.at[k]) for k, (src, dst) in enumerate(pairs)]
    for copy in copies:
        copy.start()
    for copy in copies:
        copy.wait()


def on_device(plan, xs, bc, log_decay, out_grad, news_owner, news_local):
    rows = plan.tm * plan.slots
    dma = pltpu.SemaphoreType.DMA
    vm = pltpu.VMEM
    shapes = (
        jax.ShapeDtypeStruct((64, 1024), BF16),
        jax.ShapeDtypeStruct((plan.block, 2 * L), F32),
        jax.ShapeDtypeStruct((8, L), F32),
        jax.ShapeDtypeStruct((NEWS_DEV, 64), F32),
    )
    slab = (plan.blocks, plan.block, L)
    ng, gs, nx, ny = plan.groups, plan.size, plan.x, plan.y
    scratch = [
        vm((64, 1024), BF16), vm((64, 1024), BF16), vm((1024, 2 * L), BF16),
        vm((2, 8, L, L), BF16), vm((2, 8, L, L), F32), vm((2, 9, 64, L), F32), vm((2, 8, 8, L), F32), vm((2, 8, L), F32),
        vm((2, 8, L, L), F32), vm((2, 8, plan.blocks, 2, plan.block, L), F32),
        vm((2, 8, *slab), F32), vm((2, 8, *slab), F32), vm((2, nx, plan.chunks, *slab), F32),
        vm((2, ny, plan.block, L), F32), vm((2, ny, plan.block, L), F32),
        vm((8, 64, L), F32), vm((8, 64, L), F32), vm((2, 8, L, L), BF16),
        vm((8, rows, L), BF16), vm((rows, L), F32), vm((8, L), F32), vm((8, 2 * L), F32),
        vm((gs, 72, L), F32), vm((gs, 72, L), F32), vm((2, 72, L), F32), vm((ng, 72, L), F32), vm((2, 64, L), F32),
        vm((plan.tm, plan.slots, L), F32), vm((plan.tm, plan.slots, L), F32),
        *[pltpu.SemaphoreType.REGULAR] * 3, dma((3,)),
        dma((gs,)), dma((gs,)), dma((gs,)), dma((gs,)), dma((ng, gs)), dma((ng,)),
        dma((2, 8)), dma((2, 8)), dma((2, 8)), dma((2, 8)), dma((2, ny)), dma((2, ny)),
        dma((plan.tm,)), dma((plan.tm,)),
    ]
    anywhere = pl.BlockSpec(memory_space=pl.ANY)
    vmem = pl.BlockSpec(memory_space=pltpu.VMEM)
    results = pl.pallas_call(
        functools.partial(kernel, plan),
        out_shape=shapes,
        in_specs=[anywhere] * 3 + [vmem] * 3,
        out_specs=(vmem,) * 4,
        scratch_shapes=scratch,
        compiler_params=pltpu.CompilerParams(
            collective_id=0, has_side_effects=True, vmem_limit_bytes=55000 * 1024
        ),
    )(
        xs.T, out_grad.T, bc, log_decay.reshape(8, L), news_owner.reshape(1, NQ), news_local.reshape(1, NQ)
    )
    xg, bcg, dla, news = pl.pallas_call(
        write_out,
        out_shape=shapes,
        in_specs=[anywhere] * 4,
        out_specs=(anywhere,) * 4,
        scratch_shapes=[dma((4,))],
        compiler_params=pltpu.CompilerParams(vmem_limit_bytes=2**20),
    )(*results)
    return xg.T, bcg, dla.reshape(1024, 1), news


def solution(mesh):
    tm, heads = mesh.shape["tm"], mesh.shape["head"]
    plan = Plan(tm, 3, 4, heads // 8, 8 if tm == 12 else 32)
    return jax.shard_map(
        functools.partial(on_device, plan),
        mesh=mesh,
        in_specs=(
            P("tm", "head"), P("tm", None), P("tm", "head"), P("tm", "head"), P("tm", None), P("tm", None),
        ),
        out_specs=(P("tm", "head"), P(("tm", "head"), None), P("tm", "head"), P("tm", "head")),
        check_vma=False,
    )
```
